32 devices in a mesh: sta: 8 (over z, x), seg: 4 (over y, core).
Axes of the slice: x: 2, y: 2, z: 4, core: 2. Of those that a mesh axis runs over, the one named last changes fastest.
Arguments:
- records: bfloat16 [128, 32, 4096], P('sta', 'seg'), may hold values from -6 to 6
- fir_taps: bfloat16 [32], replicated, may hold values from -1 to 1
- counts: int32 [128], replicated, may hold values from 1 to 32
- pair_blocks: int32 [16, 2], replicated, may hold values from 0 to 7, as said below
- owners: int32 [16, 1], replicated, may hold values from 0 to 7; in each aligned block of 16 rows (0 to 15, 16 to 31, ...) at most 4 rows name the same one
Outputs:
- correlation: float32 [32, 512, 256], P('sta', None, 'seg')
The draws below stay inside these ranges and needn't reach their ends.
Inputs may be any that keep to these rules, and one draw needn't show every extreme that they name: `pair_blocks`: each row names two station blocks at most one step apart in row and in column of a grid 8 blocks wide (block = 8 * row + column); every block is the first of exactly two rows. `owners`: every owner is named by 1 to 4 rows, a bound that some block reaches. A station's record is valid in segments 0 to counts - 1.
All inputs are finite; a program needn't handle non-finite values.
Results may differ from the reference program's by a relative error of at most 0.0089.
Values may be sent and summed in bfloat16 or wider, within the bound.
A program may use at most 192 MiB of HBM per device.

```python
import math
import jax
import jax.numpy as jnp
import numpy as np
from jax import lax

BLK = 16
SEGLEN = 1024
DEC = 4
TAPS = 32
NLAG = 512
CAP = 4
STATIONS = 128
SEGMENTS = 32
RAWLEN = 4096
NF = 512
PAIRS = 16
N_STA = 8


def draw_pair_blocks(key, part):
    key_first, key_second, key_col, key_row = jax.random.split(key, 4)
    first_half = jax.random.permutation(key_first, N_STA).astype(jnp.int32)
    second_half = jax.random.permutation(key_second, N_STA).astype(jnp.int32)
    first_block = jnp.concatenate([first_half, second_half]).astype(jnp.int32)
    grid_rows = N_STA // 8
    column = first_block % 8
    row_id = first_block // 8
    col_step = jax.random.randint(key_col, (PAIRS,), -1, 2).astype(jnp.int32)
    row_step = jax.random.randint(key_row, (PAIRS,), -1, 2).astype(jnp.int32)
    other = jnp.clip(row_id + row_step, 0, grid_rows - 1) * 8 + jnp.clip(column + col_step, 0, 7)
    return jnp.stack([first_block, other.astype(jnp.int32)], axis=1).astype(jnp.int32)


def plant(array, stream_key, low, high):
    dims = array.shape
    place = [jax.random.randint(jax.random.fold_in(stream_key, axis), (), 0, dims[axis]) for axis in range(len(dims))]
    array = array.at[tuple(place)].set(low)
    longest = dims.index(max(dims))
    place[longest] = (place[longest] + 1) % dims[longest]
    return array.at[tuple(place)].set(high)


def block_scale(stream_key, dims, cuts, smallest, largest):
    gain = 1.0
    for axis_at, parts in cuts:
        draws = jax.random.uniform(jax.random.fold_in(jax.random.fold_in(stream_key, 6), axis_at), (parts,), jnp.float32, smallest / len(cuts), largest / len(cuts))
        gain = gain * jnp.repeat(jnp.exp(draws), dims[axis_at] // parts).reshape((-1,) + (1,) * (len(dims) - 1 - axis_at))
    return gain


def shared_out(own_key, own, number, rows, amount, top, most, lean):
    ranking = jax.random.permutation(own_key, amount)
    packed, usual = portions_of(amount, rows * top, most, lean, True), portions_of(amount, rows * top, most, lean, False)
    places = jnp.arange(amount)

    def named(tallies, turn):
        used = int((tallies > 0).sum())
        fixed = max(1, used // 4)
        passed = fixed + (places - fixed + turn * (used - fixed)) % max(1, amount - fixed)
        return jnp.zeros((amount,), jnp.int32).at[ranking[jnp.where(places < fixed, places, passed)]].set(jnp.asarray(tallies, jnp.int32))

    tallies = jnp.where(number % 4 == 0, named(packed, number // 4), named(usual, number - number // 4 - 1))
    mixed = jax.random.permutation(jax.random.fold_in(own, 3), amount)
    giver, sink = mixed[0:amount // 2 * 2:2], mixed[1:amount // 2 * 2:2]
    room = jnp.minimum(tallies[giver] - 1, most - tallies[sink]) // 2
    room = jnp.where((giver == ranking[0]) | (sink == ranking[0]) | (tallies[sink] == 0), 0, jnp.maximum(room, 0))
    passed = jax.random.randint(jax.random.fold_in(own, 4), (amount // 2,), 0, 1 << 20) % (room + 1)
    tallies = tallies.at[giver].add(-passed).at[sink].add(passed)
    members = jnp.searchsorted(jnp.cumsum(tallies), jnp.arange(rows * top), side="right").astype(jnp.int32)
    listing = members.reshape(top, rows).T
    listing = listing[jax.random.permutation(jax.random.fold_in(own, 1), rows)]
    turn = jax.random.randint(jax.random.fold_in(own, 2), (rows, 1), 0, top)
    return jnp.take_along_axis(listing, (jnp.arange(top)[None, :] + turn) % top, axis=1)


def portions_of(number_of, total, limit, slope, full):
    weights = [(1 << 20) // math.isqrt(standing ** slope) + 1 for standing in range(1, number_of + 1)]
    largest = limit if full else min(limit, max(-(-total // number_of), total * weights[0] // sum(weights)))
    least = 1 if total - largest >= number_of - 1 else 0
    holding, rest = [largest] + [least] * (number_of - 1), total - largest - least * (number_of - 1)
    while rest > 0:
        candidates = [i for i in range(1, number_of) if holding[i] < largest] or [i for i in range(1, number_of) if holding[i] < limit]
        pool, remaining = sum([weights[i] for i in candidates]), rest
        for i in candidates:
            extra = min(limit - holding[i], max(1, remaining * weights[i] // pool), rest)
            holding[i] = holding[i] + extra
            rest = rest - extra
    return np.array(holding)


def centred(key, dims, spread, bound, shards=(), held_as=jnp.bfloat16):
    array = spread * jax.random.normal(key, dims, jnp.float32)
    if shards:
        array = array * block_scale(key, dims, shards, -0.22, 0.18)
    return jnp.clip(array, -bound, bound).astype(held_as)


def setup_inputs(seed: int = 0) -> dict:
    arg_keys = jax.random.split(jax.random.key(seed), 6)
    records = centred(arg_keys[0], (STATIONS, SEGMENTS, RAWLEN), 1.0, 6.0, ((0, 8), (1, 4)))
    fir_taps = centred(arg_keys[1], (TAPS,), TAPS ** -0.5, 1.0)
    counts = plant(jax.random.randint(arg_keys[2], (STATIONS,), 1, SEGMENTS + 1), jax.random.fold_in(arg_keys[2], 1), 1, SEGMENTS).astype(jnp.int32)
    pair_blocks = draw_pair_blocks(jax.random.fold_in(arg_keys[5], 71), 0)
    owners_keys = jax.random.split(jax.random.fold_in(arg_keys[4], 1), PAIRS // PAIRS)
    owners_turns = jax.random.permutation(jax.random.fold_in(arg_keys[4], 3), PAIRS // PAIRS)
    owners = jax.vmap(lambda own, number: shared_out(jax.random.fold_in(arg_keys[4], 2), own, number, PAIRS, N_STA, 1, CAP, 2))(owners_keys, owners_turns).reshape((PAIRS, 1))
    return dict(records=records, fir_taps=fir_taps, counts=counts, pair_blocks=pair_blocks, owners=owners)


WATER = 0.1
TINY = 1e-06

def forward_table(seglen):
    sample_pos = jnp.arange(seglen, dtype=jnp.int32)
    freq_pos = jnp.arange(seglen // 2, dtype=jnp.int32)
    phase = sample_pos[:, None] * freq_pos[None, :] % seglen
    angle = phase.astype(jnp.float32) * (2.0 * math.pi / seglen)
    return jnp.concatenate([jnp.cos(angle), -jnp.sin(angle)], axis=1).astype(jnp.bfloat16)

def inverse_table(seglen, nlag):
    freq_pos = jnp.arange(seglen // 2, dtype=jnp.int32)
    lag_pos = jnp.arange(nlag, dtype=jnp.int32) - nlag // 2
    phase = jnp.mod(freq_pos[:, None] * lag_pos[None, :], seglen)
    angle = phase.astype(jnp.float32) * (2.0 * math.pi / seglen)
    scale = 1.0 / math.sqrt(seglen // 2)
    both = jnp.stack([jnp.cos(angle) * scale, -jnp.sin(angle) * scale], axis=1)
    return both.reshape(seglen, nlag).astype(jnp.bfloat16)

def whiten(spectrum, nfreq):
    real_part = spectrum[:, :nfreq]
    imag_part = spectrum[:, nfreq:]
    magnitude = jnp.sqrt(real_part * real_part + imag_part * imag_part)
    mean_level = lax.optimization_barrier(jnp.mean(magnitude, axis=1, keepdims=True))
    divisor = magnitude + WATER * mean_level + TINY
    return spectrum / jnp.concatenate([divisor, divisor], axis=1)

def slot_tables(pair_blocks, owners, sta_count):
    owner_ids = owners[:, 0]
    position = jnp.arange(owner_ids.shape[0], dtype=jnp.int32)
    same_owner = (owner_ids[:, None] == owner_ids[None, :]) & (position[None, :] < position[:, None])
    rank_of = lax.optimization_barrier(jnp.sum(same_owner.astype(jnp.int32), axis=1))
    slot_of = owner_ids * CAP + rank_of
    slot_hit = slot_of[None, :] == jnp.arange(sta_count * CAP, dtype=jnp.int32)[:, None]
    first_block = lax.optimization_barrier(jnp.sum(jnp.where(slot_hit, pair_blocks[None, :, 0], 0), axis=1)).astype(jnp.int32)
    second_block = lax.optimization_barrier(jnp.sum(jnp.where(slot_hit, pair_blocks[None, :, 1], 0), axis=1)).astype(jnp.int32)
    live_mask = jnp.any(slot_hit, axis=1).astype(jnp.float32)
    return (first_block, second_block, live_mask)

def reference(records, fir_taps, counts, pair_blocks, owners):
    dft_table = forward_table(SEGLEN)
    taps_wide = fir_taps.astype(jnp.float32)

    def front(inputs):
        block_records, block_counts = inputs
        frames = block_records.astype(jnp.float32).reshape(BLK, SEGMENTS, SEGLEN, DEC)
        total = jnp.zeros((BLK, SEGMENTS, SEGLEN), jnp.float32)
        for tap_index in range(TAPS):
            back = tap_index // DEC
            lane = DEC - 1 - tap_index % DEC
            column = frames[:, :, :, lane]
            shifted = jnp.pad(column, ((0, 0), (0, 0), (back, 0)))[:, :, :SEGLEN]
            total = total + taps_wide[tap_index] * shifted
        samples = total.astype(jnp.bfloat16).reshape(BLK * SEGMENTS, SEGLEN)
        spectrum = jnp.dot(samples, dft_table, preferred_element_type=jnp.float32)
        white = whiten(spectrum, NF).reshape(BLK, SEGMENTS, 2 * NF)
        valid = jnp.arange(SEGMENTS, dtype=jnp.int32)[None, :] < block_counts[:, None]
        return (white * valid[:, :, None].astype(jnp.float32)).astype(jnp.bfloat16)
    whitened = lax.map(front, (records.reshape(N_STA, BLK, SEGMENTS, RAWLEN), counts.reshape(N_STA, BLK)))
    first_block, second_block, live_mask = slot_tables(pair_blocks, owners, N_STA)
    counts_grid = counts.reshape(N_STA, BLK)
    inv_table = inverse_table(SEGLEN, NLAG)

    def one_slot(inputs):
        first_one, second_one, live_one = inputs
        left = whitened[first_one].astype(jnp.float32)
        right = whitened[second_one].astype(jnp.float32)
        left_real, left_imag = (left[:, :, :NF], left[:, :, NF:])
        right_real, right_imag = (right[:, :, :NF], right[:, :, NF:])
        real_sum = jnp.einsum('isf,jsf->fij', left_real, right_real) + jnp.einsum('isf,jsf->fij', left_imag, right_imag)
        imag_sum = jnp.einsum('isf,jsf->fij', left_imag, right_real) - jnp.einsum('isf,jsf->fij', left_real, right_imag)
        common = jnp.minimum(counts_grid[first_one][:, None], counts_grid[second_one][None, :]).astype(jnp.float32)
        weight = live_one / common
        stacked = jnp.stack([real_sum * weight, imag_sum * weight], axis=1).astype(jnp.bfloat16)
        stacked = stacked.reshape(2 * NF, BLK * BLK)
        return jnp.dot(inv_table.T, stacked, preferred_element_type=jnp.float32)
    return lax.map(one_slot, (first_block, second_block, live_mask))
```

```python
import functools
import math

import jax
import jax.numpy as jnp
import ml_dtypes
import numpy as np
from jax import lax
from jax.experimental import pallas as pl
from jax.experimental.pallas import tpu as pltpu
from jax.sharding import PartitionSpec as P

DEC = 4
TAPS = 32
NLAG = 512
CAP = 4
WATER = 0.1
TINY = 1e-06
AXES = ("sta", "seg")
EARLY_SIDES = 1
VMEM = pl.BlockSpec(memory_space=pltpu.VMEM)
SMEM = pl.BlockSpec(memory_space=pltpu.SMEM)
LIMIT = 60 * 2**20
LAST_LIMIT = int(16 * 2**20)


def forward_rows(seglen):
    phase = np.arange(seglen // 2)[:, None] * np.arange(seglen)[None, :] % seglen
    angle = phase * (2.0 * math.pi / seglen)
    both = np.concatenate([np.cos(angle), -np.sin(angle)], axis=0)
    return both.astype(np.float32).astype(ml_dtypes.bfloat16)


def inverse_rows(seglen, nlag, width):
    nfreq = seglen // 2
    lag = np.arange(nlag) - nlag // 2
    angle = (lag[:, None] * np.arange(nfreq)[None, :] % seglen) * (2.0 * math.pi / seglen)
    scale = 1.0 / math.sqrt(nfreq)
    both = np.stack([np.cos(angle) * scale, -np.sin(angle) * scale], axis=1)
    both = both.reshape(nlag, 2, nfreq // width, width).transpose(0, 2, 1, 3)
    return both.reshape(nlag, 2 * nfreq).astype(np.float32).astype(ml_dtypes.bfloat16)


def spread_tables(block, segs):
    eye = np.einsum("ai,sz->aszi", np.eye(block), np.eye(segs)).reshape(block * segs, segs, block)
    some = 128 // block
    by_i = np.repeat(eye, block, axis=2).reshape(block * segs, segs, block // some, 128).transpose(2, 0, 1, 3)
    by_j = np.tile(eye, (1, 1, some))
    shape = (block * segs, segs * 128)
    return by_i.reshape((-1,) + shape).astype(ml_dtypes.bfloat16), by_j.reshape(shape).astype(ml_dtypes.bfloat16)


def fir_rows(taps_ref):
    shape = (128, 128 + 128 * DEC)
    out_pos = lax.broadcasted_iota(jnp.int32, shape, 0)
    window_pos = lax.broadcasted_iota(jnp.int32, shape, 1)
    tap_of = DEC * out_pos + DEC - 1 + 128 - window_pos
    taps = taps_ref[...].astype(jnp.float32)
    fir = jnp.zeros(shape, jnp.float32)
    for k in range(TAPS):
        fir = jnp.where(tap_of == k, taps[:, k : k + 1], fir)
    return fir.astype(jnp.bfloat16)


def decimate(fir, rec_ref, samp_ref):
    span = 128 * DEC
    for b in range(rec_ref.shape[1] // span):
        low = max(b * span - 128, 0)
        window = rec_ref[:, low : (b + 1) * span]
        kept = fir if b else fir[:, 128:]
        dec = lax.dot_general(
            kept, window, (((1,), (1,)), ((), ())), preferred_element_type=jnp.float32
        )
        samp_ref[b * 128 : (b + 1) * 128, :] = dec.astype(jnp.bfloat16)


def whitened(block, segs, counts_ref, dft_ref, samp_ref):
    rows = block * segs
    nfreq = dft_ref.shape[0] // 2
    spectrum = jnp.dot(dft_ref[...], samp_ref[...], preferred_element_type=jnp.float32)
    real, imag = spectrum[:nfreq], spectrum[nfreq:]
    magnitude = jnp.sqrt(real * real + imag * imag)
    mean_level = jnp.sum(magnitude, axis=0, keepdims=True) * (1.0 / nfreq)
    divisor = magnitude + WATER * mean_level + TINY
    lane = lax.broadcasted_iota(jnp.int32, (1, rows), 1)
    first = lax.axis_index("sta") * block
    limit = jnp.zeros((1, rows), jnp.int32)
    for i in range(block):
        limit = jnp.where(lane // segs == i, counts_ref[first + i], limit)
    valid = (lax.axis_index("seg") * segs + lane % segs < limit).astype(jnp.float32)
    gain = valid / divisor
    return real * gain, imag * gain


def front_kernel(block, segs, taps_ref, counts_ref, rec_ref, dft_ref, out_ref, samp_ref):
    decimate(fir_rows(taps_ref), rec_ref, samp_ref)
    nfreq = dft_ref.shape[0] // 2
    real, imag = whitened(block, segs, counts_ref, dft_ref, samp_ref)
    out_ref[:nfreq, :] = real.astype(jnp.bfloat16)
    out_ref[nfreq:, :] = imag.astype(jnp.bfloat16)


def whole_kernel(
    block, segs, nsta, groups, taps_ref, counts_ref, pairs_ref, owners_ref, rec_hbm, dft_hbm, by_i_hbm, by_j_hbm,
    moved_ref, rec_ref, dft_ref, by_i_ref, by_j_ref, samp_ref, white_ref, band_ref, left_ref, right_ref,
    sums_ref, made_ref, factor_ref, stack_ref, slot_ref, order_ref, table_sem, send_sem, recv_sem, send2_sem, recv2_sem,
):
    devices = nsta * groups
    lanes = block * block
    width = white_ref.shape[1] // 2
    npairs = owners_ref.shape[1]
    own_sta, own_seg = lax.axis_index("sta"), lax.axis_index("seg")
    me = own_sta * groups + own_seg

    def place(d):
        return {"sta": d // groups, "seg": d % groups}

    tables = [
        pltpu.make_async_copy(src, dst, table_sem.at[n])
        for n, (src, dst) in enumerate(
            (
                (rec_hbm, rec_ref),
                (dft_hbm, dft_ref),
                (by_i_hbm, by_i_ref),
                (by_j_hbm, by_j_ref),
            )
        )
    ]
    for table in tables:
        table.start()
    barrier = pltpu.get_barrier_semaphore()

    @pl.loop(1, devices)
    def _(k):
        pl.semaphore_signal(
            barrier, inc=1, device_id=place(lax.rem(me + k, devices)), device_id_type=pl.DeviceIdType.MESH
        )

    fir = fir_rows(taps_ref)
    tables[0].wait()
    decimate(fir, rec_ref, samp_ref)
    tables[1].wait()
    real, imag = whitened(block, segs, counts_ref, dft_ref, samp_ref)
    for d in range(devices):
        both = jnp.concatenate([part[d * width : (d + 1) * width] for part in (real, imag)], axis=0)
        white_ref[d] = both.astype(jnp.bfloat16)
    pl.semaphore_wait(barrier, devices - 1)

    def band_copy(to, landed):
        return pltpu.make_async_remote_copy(
            src_ref=white_ref.at[to],
            dst_ref=band_ref.at[landed],
            send_sem=send_sem.at[to],
            recv_sem=recv_sem.at[landed],
            device_id=place(to),
            device_id_type=pl.DeviceIdType.MESH,
        )

    def stack_copy(to, landed):
        return pltpu.make_async_remote_copy(
            src_ref=stack_ref.at[to],
            dst_ref=moved_ref.at[landed],
            send_sem=send2_sem.at[to],
            recv_sem=recv2_sem.at[landed],
            device_id=place(to),
            device_id_type=pl.DeviceIdType.MESH,
        )

    @pl.loop(1, devices)
    def _(k):
        band_copy(lax.rem(me + k, devices), me).start()

    band_ref[me] = white_ref[me]

    many, few = nsta // 2, nsta - 2
    near_half = own_sta // many
    far_half = 1 - near_half
    firsts = [pairs_ref[0, p] for p in range(npairs)]
    seconds = [pairs_ref[1, p] for p in range(npairs)]
    inside = [
        ((first // many == near_half) & (second // many == near_half)).astype(jnp.int32)
        for first, second in zip(firsts, seconds)
    ]
    count = sum(inside)
    before = jnp.int32(0)
    places, slots = [], []
    for p in range(npairs):
        places.append(jnp.where(inside[p] == 1, before, count + p - before))
        before = before + inside[p]
        rank = jnp.int32(0)
        for q in range(p):
            rank = rank + (owners_ref[0, q] == owners_ref[0, p]).astype(jnp.int32)
        slots.append(owners_ref[0, p] * CAP + rank)
    for q in range(nsta * CAP):
        pair = jnp.int32(npairs)
        for p in range(npairs):
            pair = jnp.where(slots[p] == q, places[p], pair)
        slot_ref[q] = pair
    for q in range(npairs):
        pair = jnp.int32(0)
        for p in range(1, npairs):
            pair = jnp.where(places[p] == q, p, pair)
        order_ref[q] = pair
    made_ref[npairs] = jnp.zeros(made_ref.shape[1:], jnp.bfloat16)

    halves = lanes // 128
    per_half = 128 // block
    lane = lax.broadcasted_iota(jnp.int32, (1, 128), 1)
    low = lax.broadcasted_iota(jnp.int32, (2 * width, 128), 1) < 64
    sides = [lax.rem(own_seg // 2 + 1 + turn, halves) for turn in range(halves)]

    @pl.loop(0, npairs)
    def _(p):
        first, second = pairs_ref[0, p], pairs_ref[1, p]
        right_count = jnp.zeros((1, 128), jnp.int32)
        for i in range(block):
            right_count = jnp.where(lane % block == i, counts_ref[second * block + i], right_count)
        for side in range(halves):
            left_count = jnp.zeros((1, 128), jnp.int32)
            for i in range(per_half):
                here = counts_ref[first * block + side * per_half + i]
                left_count = jnp.where(lane // block == i, here, left_count)
            factor = 1.0 / jnp.minimum(left_count, right_count).astype(jnp.float32)
            factor_ref[side, p] = jnp.broadcast_to(factor, factor_ref.shape[2:])

    def expand(half, table, into):
        held = band_ref[pl.ds(half * many * groups, many * groups)].reshape(many * groups * 2 * width, -1)
        for s in range(0, segs, 2):
            wide = jnp.dot(held, table[:, s * 128 : s * 128 + 256], preferred_element_type=jnp.float32)
            wide = wide.reshape(many, groups * 2 * width, 256)
            into[pl.ds(half * many, many), s] = wide[:, :, :128]
            into[pl.ds(half * many, many), s + 1] = wide[:, :, 128:]

    def cross(side, low_pair, high_pair):
        @pl.loop(low_pair, high_pair)
        def _(n):
            p = order_ref[n]
            first, second = pairs_ref[0, p], pairs_ref[1, p]
            factor = factor_ref[side, p]
            for r in range(0, width, 8):
                sums = [jnp.zeros((8, 128), jnp.float32) for _ in range(8)]
                for s in range(segs):
                    for g in range(groups):
                        at = g * 2 * width + r
                        lr = left_ref[side, first, s, at : at + 8, :]
                        li = left_ref[side, first, s, at + width : at + width + 8, :]
                        rr = right_ref[second, s, at : at + 8, :]
                        ri = right_ref[second, s, at + width : at + width + 8, :]
                        m = g % 2 * 4
                        sums[m] += lr * rr
                        sums[m + 1] += li * ri
                        sums[m + 2] += li * rr
                        sums[m + 3] += lr * ri
                sums = [sums[m] + sums[m + 4] for m in range(4)]
                sums_ref[side, n, r : r + 8] = (sums[0] + sums[1]) * factor
                sums_ref[side, n, width + r : width + r + 8] = (sums[2] - sums[3]) * factor

    tables[2].wait()
    tables[3].wait()

    @pl.loop(1, many * groups)
    def _(k):
        src = near_half * many * groups + lax.rem(me + k, many * groups)
        band_copy(src, src).wait_recv()

    expand(near_half, by_j_ref, right_ref)
    for side in sides[:EARLY_SIDES]:
        expand(near_half, by_i_ref.at[side], left_ref.at[side])
        cross(side, 0, few)

    @pl.loop(0, many * groups)
    def _(k):
        src = far_half * many * groups + lax.rem(me + k, many * groups)
        band_copy(src, src).wait_recv()

    expand(far_half, by_j_ref, right_ref)
    for turn, side in enumerate(sides):
        expand(far_half, by_i_ref.at[side], left_ref.at[side])
        if turn >= EARLY_SIDES:
            expand(near_half, by_i_ref.at[side], left_ref.at[side])
            cross(side, 0, few)
        cross(side, few, npairs)
        every = sums_ref[side].reshape(npairs * 2 * width, 128)
        for n, turned in enumerate((every, pltpu.roll(every, 64, 1))):
            made_ref[:npairs, n] = turned.astype(jnp.bfloat16).reshape(npairs, 2 * width, 128)
        for k in range(nsta):
            owner = lax.rem(own_sta + 1 + k, nsta)
            to = owner * groups + 2 * side
            for half in range(CAP // 2):
                even, odd = slot_ref[owner * CAP + 2 * half], slot_ref[owner * CAP + 2 * half + 1]
                stack_ref[to, half] = jnp.where(low, made_ref[even, 0], made_ref[odd, 1])
                stack_ref[to + 1, half] = jnp.where(low, made_ref[even, 1], made_ref[odd, 0])

        @pl.loop(0, 2 * nsta)
        def _(k):
            to = lax.rem(own_sta + 1 + k // 2, nsta) * groups + 2 * side + k % 2

            @pl.when(to != me)
            def _():
                stack_copy(to, me).start()

    own = pltpu.make_async_copy(stack_ref.at[me], moved_ref.at[me], table_sem.at[0])
    own.start()

    @pl.loop(1, devices)
    def _(k):
        src = lax.rem(me + k, devices)
        stack_copy(src, src).wait_recv()

    @pl.loop(1, devices)
    def _(k):
        to = lax.rem(me + k, devices)
        band_copy(to, me).wait_send()
        stack_copy(to, me).wait_send()

    own.wait()


def owner_kernel(inv_ref, moved_hbm, out_hbm, moved_ref, out_ref, in_sem, out_sem):
    halves = range(CAP // 2)
    loads = [pltpu.make_async_copy(moved_hbm.at[:, h], moved_ref.at[h], in_sem.at[h]) for h in halves]
    stores = [
        pltpu.make_async_copy(out_ref.at[pl.ds(2 * h, 2)], out_hbm.at[pl.ds(2 * h, 2)], out_sem.at[h]) for h in halves
    ]
    for load in loads:
        load.start()
    for h in halves:
        loads[h].wait()
        held = moved_ref[h].reshape(-1, 128)
        result = lax.dot_general(
            held, inv_ref[...], (((0,), (0,)), ((), ())), preferred_element_type=jnp.float32
        )
        out_ref[2 * h] = result[:64]
        out_ref[2 * h + 1] = result[64:]
        stores[h].start()
    for store in stores:
        store.wait()


def cross_plain(bands, counts, pair_blocks, owners, nsta, groups, segs, width):
    owner_ids = owners[:, 0]
    position = jnp.arange(owner_ids.shape[0], dtype=jnp.int32)
    same = (owner_ids[:, None] == owner_ids[None, :]) & (position[None, :] < position[:, None])
    slot_of = owner_ids * CAP + jnp.sum(same.astype(jnp.int32), axis=1)
    block = counts.shape[0] // nsta
    hit = (slot_of[:, None] == jnp.arange(nsta * CAP, dtype=jnp.int32)[None, :]).astype(jnp.bfloat16)
    blocks = jnp.arange(nsta, dtype=jnp.int32)
    data = bands.reshape(nsta, groups, 2, width, block, segs)
    grid = counts.reshape(nsta, block).astype(jnp.float32)
    sides, limits = [], []
    for side in range(2):
        pick = (pair_blocks[:, side][:, None] == blocks[None, :]).astype(jnp.bfloat16)
        chosen = jnp.einsum("pn,ngufis->pgufis", pick, data, preferred_element_type=jnp.float32)
        sides.append(chosen.astype(jnp.bfloat16))
        limits.append(jnp.sum(jnp.where(pick[:, :, None] > 0, grid[None], 0.0), axis=1))
    left, right = sides
    common = jnp.minimum(limits[0][:, None, :, None], limits[1][:, None, None, :])
    dot = functools.partial(jnp.einsum, "pgfis,pgfjs->pfij", preferred_element_type=jnp.float32)
    real = dot(left[:, :, 0], right[:, :, 0]) + dot(left[:, :, 1], right[:, :, 1])
    imag = dot(left[:, :, 1], right[:, :, 0]) - dot(left[:, :, 0], right[:, :, 1])
    made = jnp.stack([real / common, imag / common], axis=1).astype(jnp.bfloat16)
    slots = jnp.einsum("pq,pufl->qufl", hit, made.reshape(made.shape[:3] + (block * block,)), preferred_element_type=jnp.float32)
    slots = slots.astype(jnp.bfloat16).reshape(nsta, CAP, 2, width, groups, block * block // groups)
    return slots.transpose(0, 4, 2, 3, 1, 5).reshape(nsta * groups, 2 * width, CAP * block * block // groups)


def last_kernel(inv_ref, stack_ref, out_ref):
    result = jnp.dot(inv_ref[...], stack_ref[...], preferred_element_type=jnp.float32)
    lanes = out_ref.shape[2]
    for c in range(out_ref.shape[0]):
        out_ref[c] = result[:, c * lanes : (c + 1) * lanes]


def local(records, fir_taps, counts, pair_blocks, owners):
    block, segs, raw = records.shape
    nsta, groups = lax.axis_size("sta"), lax.axis_size("seg")
    devices = nsta * groups
    seglen = raw // DEC
    nfreq = seglen // 2
    width = nfreq // devices
    rows = block * segs
    lanes = block * block
    fast = width % 16 == 0 and nsta == 8 and owners.shape[0] == 2 * nsta and lanes // groups == 64 and rows == 128
    bf16 = jnp.bfloat16

    taps = fir_taps.reshape(1, TAPS)
    flat = records.reshape(rows, raw)
    forward = jnp.asarray(forward_rows(seglen))
    inverse = inverse_rows(seglen, NLAG, width)
    if fast:
        by_i, by_j = (jnp.asarray(t) for t in spread_tables(block, segs))
        operands = (flat, forward, by_i, by_j)
        spread = (nsta, segs, groups * 2 * width, 128)
        bands = pltpu.VMEM((devices, 2 * width, rows), bf16)
        stacks = pltpu.VMEM((devices, CAP // 2, 2 * width, 128), bf16)
        moved = pl.pallas_call(
            functools.partial(whole_kernel, block, segs, nsta, groups),
            out_shape=jax.ShapeDtypeStruct((devices, CAP // 2, 2 * width, 128), bf16),
            in_specs=[VMEM] + [SMEM] * 3 + [pl.BlockSpec(memory_space=pl.ANY)] * 4,
            out_specs=pl.BlockSpec(memory_space=pl.ANY),
            scratch_shapes=[
                *(pltpu.VMEM(x.shape, bf16) for x in operands),
                pltpu.VMEM((seglen, rows), bf16),
                bands,
                bands,
                pltpu.VMEM((lanes // 128,) + spread, jnp.float32),
                pltpu.VMEM(spread, jnp.float32),
                pltpu.VMEM((lanes // 128, owners.shape[0], 2 * width, 128), jnp.float32),
                pltpu.VMEM((owners.shape[0] + 1, 2, 2 * width, 128), bf16),
                pltpu.VMEM((lanes // 128, owners.shape[0], 8, 128), jnp.float32),
                stacks,
                pltpu.SMEM((nsta * CAP,), jnp.int32),
                pltpu.SMEM((owners.shape[0],), jnp.int32),
                pltpu.SemaphoreType.DMA((4,)),
                *(pltpu.SemaphoreType.DMA((devices)) for _ in range(4)),
            ],
            compiler_params=pltpu.CompilerParams(
                vmem_limit_bytes=LIMIT, collective_id=0, has_side_effects=True
            ),
            name="whole",
        )(taps, counts, pair_blocks.T, owners.T, *operands)
        by_lane = pl.pallas_call(
            owner_kernel,
            out_shape=jax.ShapeDtypeStruct((CAP, lanes // groups, NLAG), jnp.float32),
            in_specs=[VMEM, pl.BlockSpec(memory_space=pl.ANY)],
            out_specs=pl.BlockSpec(memory_space=pl.ANY),
            scratch_shapes=[
                pltpu.VMEM((CAP // 2, devices, 2 * width, 128), bf16),
                pltpu.VMEM((CAP, lanes // groups, NLAG), jnp.float32),
                pltpu.SemaphoreType.DMA((CAP // 2,)),
                pltpu.SemaphoreType.DMA((CAP // 2,)),
            ],
            compiler_params=pltpu.CompilerParams(vmem_limit_bytes=LAST_LIMIT),
            name="owner",
        )(jnp.asarray(inverse.T), moved)
        return by_lane.transpose(0, 2, 1)
    params = pltpu.CompilerParams(vmem_limit_bytes=LIMIT)
    white = pl.pallas_call(
        functools.partial(front_kernel, block, segs),
        out_shape=jax.ShapeDtypeStruct((2 * nfreq, rows), bf16),
        in_specs=[VMEM, SMEM, VMEM, VMEM],
        out_specs=VMEM,
        scratch_shapes=[pltpu.VMEM((seglen, rows), bf16)],
        compiler_params=params,
        name="front",
    )(taps, counts, flat, forward)
    white = white.reshape(2, devices, width, rows).transpose(1, 0, 2, 3)
    bands = lax.all_to_all(white.reshape(devices, 2 * width, rows), AXES, 0, 0, tiled=True)
    stacked = cross_plain(bands, counts, pair_blocks, owners, nsta, groups, segs, width)
    moved = lax.all_to_all(stacked, AXES, 0, 0, tiled=True)
    return pl.pallas_call(
        last_kernel,
        out_shape=jax.ShapeDtypeStruct((CAP, NLAG, lanes // groups), jnp.float32),
        in_specs=[VMEM, VMEM],
        out_specs=VMEM,
        compiler_params=params,
        name="last",
    )(jnp.asarray(inverse), moved.reshape(2 * nfreq, CAP * lanes // groups))


def solution(mesh):
    in_specs = (P("sta", "seg", None), P(), P(), P(), P())
    out_specs = P("sta", None, "seg")
    return jax.shard_map(local, mesh=mesh, in_specs=in_specs, out_specs=out_specs, check_vma=False)
```

```python
import functools
import math

import jax
import jax.numpy as jnp
import ml_dtypes
import numpy as np
from jax import lax
from jax.experimental import pallas as pl
from jax.experimental.pallas import tpu as pltpu
from jax.sharding import PartitionSpec as P

DEC = 4
TAPS = 32
NLAG = 512
CAP = 4
WATER = 0.1
TINY = 1e-06
AXES = ("sta", "seg")
EARLY_SIDES = 1
VMEM = pl.BlockSpec(memory_space=pltpu.VMEM)
SMEM = pl.BlockSpec(memory_space=pltpu.SMEM)
LIMIT = 60 * 2**20
LAST_LIMIT = int(16 * 2**20)


def forward_rows(seglen):
    phase = np.arange(seglen // 2)[:, None] * np.arange(seglen)[None, :] % seglen
    angle = phase * (2.0 * math.pi / seglen)
    both = np.concatenate([np.cos(angle), -np.sin(angle)], axis=0)
    return both.astype(np.float32).astype(ml_dtypes.bfloat16)


def inverse_rows(seglen, nlag, width):
    nfreq = seglen // 2
    lag = np.arange(nlag) - nlag // 2
    angle = (lag[:, None] * np.arange(nfreq)[None, :] % seglen) * (2.0 * math.pi / seglen)
    scale = 1.0 / math.sqrt(nfreq)
    both = np.stack([np.cos(angle) * scale, -np.sin(angle) * scale], axis=1)
    both = both.reshape(nlag, 2, nfreq // width, width).transpose(0, 2, 1, 3)
    return both.reshape(nlag, 2 * nfreq).astype(np.float32).astype(ml_dtypes.bfloat16)


def spread_tables(block, segs):
    eye = np.einsum("ai,sz->aszi", np.eye(block), np.eye(segs)).reshape(block * segs, segs, block)
    some = 128 // block
    by_i = np.repeat(eye, block, axis=2).reshape(block * segs, segs, block // some, 128).transpose(2, 0, 1, 3)
    by_j = np.tile(eye, (1, 1, some))
    shape = (block * segs, segs * 128)
    return by_i.reshape((-1,) + shape).astype(ml_dtypes.bfloat16), by_j.reshape(shape).astype(ml_dtypes.bfloat16)


def fir_rows(taps_ref):
    tap_of = (
        DEC * lax.broadcasted_iota(jnp.int32, (64, 128), 0) - lax.broadcasted_iota(jnp.int32, (64, 128), 1) - 61
    )
    taps = taps_ref[...].astype(jnp.float32)
    tile = jnp.zeros((64, 128), jnp.float32)
    for k in range(TAPS):
        tile = jnp.where(tap_of == k, taps[:, k : k + 1], tile)
    tile = tile.astype(jnp.bfloat16)
    columns = []
    for t in range(1 + DEC):
        top = 32 * t - 48
        low, high = max(top, 0), min(top + 64, 128)
        rows = [tile[low - top : high - top]]
        if low:
            rows.insert(0, jnp.zeros((low, 128), jnp.bfloat16))
        if high < 128:
            rows.append(jnp.zeros((128 - high, 128), jnp.bfloat16))
        columns.append(jnp.concatenate(rows, axis=0))
    return jnp.concatenate(columns, axis=1)


def decimate(fir, rec_ref, samp_ref):
    span = 128 * DEC
    for b in range(rec_ref.shape[1] // span):
        low = max(b * span - 128, 0)
        window = rec_ref[:, low : (b + 1) * span]
        kept = fir if b else fir[:, 128:]
        dec = lax.dot_general(
            kept, window, (((1,), (1,)), ((), ())), preferred_element_type=jnp.float32
        )
        samp_ref[b * 128 : (b + 1) * 128, :] = dec.astype(jnp.bfloat16)


def whitened(block, segs, counts_ref, dft_ref, samp_ref):
    rows = block * segs
    nfreq = dft_ref.shape[0] // 2
    spectrum = jnp.dot(dft_ref[...], samp_ref[...], preferred_element_type=jnp.float32)
    real, imag = spectrum[:nfreq], spectrum[nfreq:]
    magnitude = jnp.sqrt(real * real + imag * imag)
    mean_level = jnp.sum(magnitude, axis=0, keepdims=True) * (1.0 / nfreq)
    divisor = magnitude + WATER * mean_level + TINY
    lane = lax.broadcasted_iota(jnp.int32, (1, rows), 1)
    first = lax.axis_index("sta") * block
    limit = jnp.zeros((1, rows), jnp.int32)
    for i in range(block):
        limit = jnp.where(lane // segs == i, counts_ref[first + i], limit)
    valid = (lax.axis_index("seg") * segs + lane % segs < limit).astype(jnp.float32)
    gain = valid / divisor
    return real * gain, imag * gain


def front_kernel(block, segs, taps_ref, counts_ref, rec_ref, dft_ref, out_ref, samp_ref):
    decimate(fir_rows(taps_ref), rec_ref, samp_ref)
    nfreq = dft_ref.shape[0] // 2
    real, imag = whitened(block, segs, counts_ref, dft_ref, samp_ref)
    out_ref[:nfreq, :] = real.astype(jnp.bfloat16)
    out_ref[nfreq:, :] = imag.astype(jnp.bfloat16)


def whole_kernel(
    block, segs, nsta, groups, taps_ref, counts_ref, pairs_ref, owners_ref, rec_hbm, dft_hbm, by_i_hbm, by_j_hbm,
    moved_ref, rec_ref, dft_ref, by_i_ref, by_j_ref, samp_ref, white_ref, band_ref, left_ref, right_ref,
    sums_ref, made_ref, factor_ref, stack_ref, slot_ref, order_ref, table_sem, send_sem, recv_sem, send2_sem, recv2_sem,
):
    devices = nsta * groups
    lanes = block * block
    width = white_ref.shape[1] // 2
    npairs = owners_ref.shape[1]
    own_sta, own_seg = lax.axis_index("sta"), lax.axis_index("seg")
    me = own_sta * groups + own_seg

    def place(d):
        return {"sta": d // groups, "seg": d % groups}

    tables = [
        pltpu.make_async_copy(src, dst, table_sem.at[n])
        for n, (src, dst) in enumerate(
            (
                (rec_hbm, rec_ref),
                (dft_hbm, dft_ref),
                (by_i_hbm, by_i_ref),
                (by_j_hbm, by_j_ref),
            )
        )
    ]
    for table in tables:
        table.start()
    barrier = pltpu.get_barrier_semaphore()

    @pl.loop(1, devices)
    def _(k):
        pl.semaphore_signal(
            barrier, inc=1, device_id=place(lax.rem(me + k, devices)), device_id_type=pl.DeviceIdType.MESH
        )

    fir = fir_rows(taps_ref)
    tables[0].wait()
    decimate(fir, rec_ref, samp_ref)
    tables[1].wait()
    real, imag = whitened(block, segs, counts_ref, dft_ref, samp_ref)
    for d in range(devices):
        both = jnp.concatenate([part[d * width : (d + 1) * width] for part in (real, imag)], axis=0)
        white_ref[d] = both.astype(jnp.bfloat16)
    pl.semaphore_wait(barrier, devices - 1)

    def band_copy(to, landed):
        return pltpu.make_async_remote_copy(
            src_ref=white_ref.at[to],
            dst_ref=band_ref.at[landed],
            send_sem=send_sem.at[to],
            recv_sem=recv_sem.at[landed],
            device_id=place(to),
            device_id_type=pl.DeviceIdType.MESH,
        )

    def stack_copy(to, landed):
        return pltpu.make_async_remote_copy(
            src_ref=stack_ref.at[to],
            dst_ref=moved_ref.at[landed],
            send_sem=send2_sem.at[to],
            recv_sem=recv2_sem.at[landed],
            device_id=place(to),
            device_id_type=pl.DeviceIdType.MESH,
        )

    @pl.loop(1, devices)
    def _(k):
        band_copy(lax.rem(me + k, devices), me).start()

    band_ref[me] = white_ref[me]

    many, few = nsta // 2, nsta - 2
    near_half = own_sta // many
    far_half = 1 - near_half
    firsts = [pairs_ref[0, p] for p in range(npairs)]
    seconds = [pairs_ref[1, p] for p in range(npairs)]
    inside = [
        ((first // many == near_half) & (second // many == near_half)).astype(jnp.int32)
        for first, second in zip(firsts, seconds)
    ]
    count = sum(inside)
    before = jnp.int32(0)
    places, slots = [], []
    for p in range(npairs):
        places.append(jnp.where(inside[p] == 1, before, count + p - before))
        before = before + inside[p]
        rank = jnp.int32(0)
        for q in range(p):
            rank = rank + (owners_ref[0, q] == owners_ref[0, p]).astype(jnp.int32)
        slots.append(owners_ref[0, p] * CAP + rank)
    for q in range(nsta * CAP):
        pair = jnp.int32(npairs)
        for p in range(npairs):
            pair = jnp.where(slots[p] == q, places[p], pair)
        slot_ref[q] = pair
    for q in range(npairs):
        pair = jnp.int32(0)
        for p in range(1, npairs):
            pair = jnp.where(places[p] == q, p, pair)
        order_ref[q] = pair
    made_ref[npairs] = jnp.zeros(made_ref.shape[1:], jnp.bfloat16)

    halves = lanes // 128
    per_half = 128 // block
    lane = lax.broadcasted_iota(jnp.int32, (1, 128), 1)
    low = lax.broadcasted_iota(jnp.int32, (2 * width, 128), 1) < 64
    sides = list(range(halves))

    @pl.loop(0, npairs)
    def _(p):
        first, second = pairs_ref[0, p], pairs_ref[1, p]
        right_count = jnp.zeros((1, 128), jnp.int32)
        for i in range(block):
            right_count = jnp.where(lane % block == i, counts_ref[second * block + i], right_count)
        for side in range(halves):
            left_count = jnp.zeros((1, 128), jnp.int32)
            for i in range(per_half):
                here = counts_ref[first * block + side * per_half + i]
                left_count = jnp.where(lane // block == i, here, left_count)
            factor = 1.0 / jnp.minimum(left_count, right_count).astype(jnp.float32)
            factor_ref[side, p] = jnp.broadcast_to(factor, factor_ref.shape[2:])

    def expand(half, table, into):
        held = band_ref[pl.ds(half * many * groups, many * groups)].reshape(many * groups * 2 * width, -1)
        for s in range(0, segs, 2):
            wide = jnp.dot(held, table[:, s * 128 : s * 128 + 256], preferred_element_type=jnp.float32)
            wide = wide.reshape(many, groups * 2 * width, 256)
            into[pl.ds(half * many, many), s] = wide[:, :, :128]
            into[pl.ds(half * many, many), s + 1] = wide[:, :, 128:]

    def cross(side, low_pair, high_pair):
        @pl.loop(low_pair, high_pair)
        def _(n):
            p = order_ref[n]
            first, second = pairs_ref[0, p], pairs_ref[1, p]
            factor = factor_ref[side, p]
            for r in range(0, width, 8):
                sums = [jnp.zeros((8, 128), jnp.float32) for _ in range(8)]
                for s in range(segs):
                    for g in range(groups):
                        at = g * 2 * width + r
                        lr = left_ref[side, first, s, at : at + 8, :]
                        li = left_ref[side, first, s, at + width : at + width + 8, :]
                        rr = right_ref[second, s, at : at + 8, :]
                        ri = right_ref[second, s, at + width : at + width + 8, :]
                        m = g % 2 * 4
                        sums[m] += lr * rr
                        sums[m + 1] += li * ri
                        sums[m + 2] += li * rr
                        sums[m + 3] += lr * ri
                sums = [sums[m] + sums[m + 4] for m in range(4)]
                sums_ref[side, n, r : r + 8] = (sums[0] + sums[1]) * factor
                sums_ref[side, n, width + r : width + r + 8] = (sums[2] - sums[3]) * factor

    tables[2].wait()
    tables[3].wait()

    @pl.loop(1, many * groups)
    def _(k):
        src = near_half * many * groups + lax.rem(me + k, many * groups)
        band_copy(src, src).wait_recv()

    expand(near_half, by_j_ref, right_ref)
    for side in sides[:EARLY_SIDES]:
        expand(near_half, by_i_ref.at[side], left_ref.at[side])
        cross(side, 0, few)

    @pl.loop(0, many * groups)
    def _(k):
        src = far_half * many * groups + lax.rem(me + k, many * groups)
        band_copy(src, src).wait_recv()

    expand(far_half, by_j_ref, right_ref)
    for turn, side in enumerate(sides):
        expand(far_half, by_i_ref.at[side], left_ref.at[side])
        if turn >= EARLY_SIDES:
            expand(near_half, by_i_ref.at[side], left_ref.at[side])
            cross(side, 0, few)
        cross(side, few, npairs)
        every = sums_ref[side].reshape(npairs * 2 * width, 128)
        for n, turned in enumerate((every, pltpu.roll(every, 64, 1))):
            made_ref[:npairs, n] = turned.astype(jnp.bfloat16).reshape(npairs, 2 * width, 128)
        for k in range(nsta):
            owner = lax.rem(own_sta + 1 + k, nsta)
            to = owner * groups + 2 * side
            for half in range(CAP // 2):
                even, odd = slot_ref[owner * CAP + 2 * half], slot_ref[owner * CAP + 2 * half + 1]
                stack_ref[to, half] = jnp.where(low, made_ref[even, 0], made_ref[odd, 1])
                stack_ref[to + 1, half] = jnp.where(low, made_ref[even, 1], made_ref[odd, 0])

        @pl.loop(0, 2 * nsta)
        def _(k):
            to = lax.rem(own_sta + 1 + k // 2, nsta) * groups + 2 * side + k % 2

            @pl.when(to != me)
            def _():
                stack_copy(to, me).start()

    own = pltpu.make_async_copy(stack_ref.at[me], moved_ref.at[me], table_sem.at[0])
    own.start()

    @pl.loop(1, devices)
    def _(k):
        src = lax.rem(me + k, devices)
        stack_copy(src, src).wait_recv()

    @pl.loop(1, devices)
    def _(k):
        to = lax.rem(me + k, devices)
        band_copy(to, me).wait_send()
        stack_copy(to, me).wait_send()

    own.wait()


def owner_kernel(inv_ref, moved_hbm, out_hbm, moved_ref, out_ref, in_sem, out_sem):
    halves = range(CAP // 2)
    loads = [pltpu.make_async_copy(moved_hbm.at[:, h], moved_ref.at[h], in_sem.at[h]) for h in halves]
    stores = [
        pltpu.make_async_copy(out_ref.at[pl.ds(2 * h, 2)], out_hbm.at[pl.ds(2 * h, 2)], out_sem.at[h]) for h in halves
    ]
    for load in loads:
        load.start()
    for h in halves:
        loads[h].wait()
        held = moved_ref[h].reshape(-1, 128)
        result = lax.dot_general(
            held, inv_ref[...], (((0,), (0,)), ((), ())), preferred_element_type=jnp.float32
        )
        out_ref[2 * h] = result[:64]
        out_ref[2 * h + 1] = result[64:]
        stores[h].start()
    for store in stores:
        store.wait()


def cross_plain(bands, counts, pair_blocks, owners, nsta, groups, segs, width):
    owner_ids = owners[:, 0]
    position = jnp.arange(owner_ids.shape[0], dtype=jnp.int32)
    same = (owner_ids[:, None] == owner_ids[None, :]) & (position[None, :] < position[:, None])
    slot_of = owner_ids * CAP + jnp.sum(same.astype(jnp.int32), axis=1)
    block = counts.shape[0] // nsta
    hit = (slot_of[:, None] == jnp.arange(nsta * CAP, dtype=jnp.int32)[None, :]).astype(jnp.bfloat16)
    blocks = jnp.arange(nsta, dtype=jnp.int32)
    data = bands.reshape(nsta, groups, 2, width, block, segs)
    grid = counts.reshape(nsta, block).astype(jnp.float32)
    sides, limits = [], []
    for side in range(2):
        pick = (pair_blocks[:, side][:, None] == blocks[None, :]).astype(jnp.bfloat16)
        chosen = jnp.einsum("pn,ngufis->pgufis", pick, data, preferred_element_type=jnp.float32)
        sides.append(chosen.astype(jnp.bfloat16))
        limits.append(jnp.sum(jnp.where(pick[:, :, None] > 0, grid[None], 0.0), axis=1))
    left, right = sides
    common = jnp.minimum(limits[0][:, None, :, None], limits[1][:, None, None, :])
    dot = functools.partial(jnp.einsum, "pgfis,pgfjs->pfij", preferred_element_type=jnp.float32)
    real = dot(left[:, :, 0], right[:, :, 0]) + dot(left[:, :, 1], right[:, :, 1])
    imag = dot(left[:, :, 1], right[:, :, 0]) - dot(left[:, :, 0], right[:, :, 1])
    made = jnp.stack([real / common, imag / common], axis=1).astype(jnp.bfloat16)
    slots = jnp.einsum("pq,pufl->qufl", hit, made.reshape(made.shape[:3] + (block * block,)), preferred_element_type=jnp.float32)
    slots = slots.astype(jnp.bfloat16).reshape(nsta, CAP, 2, width, groups, block * block // groups)
    return slots.transpose(0, 4, 2, 3, 1, 5).reshape(nsta * groups, 2 * width, CAP * block * block // groups)


def last_kernel(inv_ref, stack_ref, out_ref):
    result = jnp.dot(inv_ref[...], stack_ref[...], preferred_element_type=jnp.float32)
    lanes = out_ref.shape[2]
    for c in range(out_ref.shape[0]):
        out_ref[c] = result[:, c * lanes : (c + 1) * lanes]


def local(records, fir_taps, counts, pair_blocks, owners):
    block, segs, raw = records.shape
    nsta, groups = lax.axis_size("sta"), lax.axis_size("seg")
    devices = nsta * groups
    seglen = raw // DEC
    nfreq = seglen // 2
    width = nfreq // devices
    rows = block * segs
    lanes = block * block
    fast = width % 16 == 0 and nsta == 8 and owners.shape[0] == 2 * nsta and lanes // groups == 64 and rows == 128
    bf16 = jnp.bfloat16

    taps = fir_taps.reshape(1, TAPS)
    flat = records.reshape(rows, raw)
    forward = jnp.asarray(forward_rows(seglen))
    inverse = inverse_rows(seglen, NLAG, width)
    if fast:
        by_i, by_j = (jnp.asarray(t) for t in spread_tables(block, segs))
        operands = (flat, forward, by_i, by_j)
        spread = (nsta, segs, groups * 2 * width, 128)
        bands = pltpu.VMEM((devices, 2 * width, rows), bf16)
        stacks = pltpu.VMEM((devices, CAP // 2, 2 * width, 128), bf16)
        moved = pl.pallas_call(
            functools.partial(whole_kernel, block, segs, nsta, groups),
            out_shape=jax.ShapeDtypeStruct((devices, CAP // 2, 2 * width, 128), bf16),
            in_specs=[VMEM] + [SMEM] * 3 + [pl.BlockSpec(memory_space=pl.ANY)] * 4,
            out_specs=pl.BlockSpec(memory_space=pl.ANY),
            scratch_shapes=[
                *(pltpu.VMEM(x.shape, bf16) for x in operands),
                pltpu.VMEM((seglen, rows), bf16),
                bands,
                bands,
                pltpu.VMEM((lanes // 128,) + spread, jnp.float32),
                pltpu.VMEM(spread, jnp.float32),
                pltpu.VMEM((lanes // 128, owners.shape[0], 2 * width, 128), jnp.float32),
                pltpu.VMEM((owners.shape[0] + 1, 2, 2 * width, 128), bf16),
                pltpu.VMEM((lanes // 128, owners.shape[0], 8, 128), jnp.float32),
                stacks,
                pltpu.SMEM((nsta * CAP,), jnp.int32),
                pltpu.SMEM((owners.shape[0],), jnp.int32),
                pltpu.SemaphoreType.DMA((4,)),
                *(pltpu.SemaphoreType.DMA((devices)) for _ in range(4)),
            ],
            compiler_params=pltpu.CompilerParams(
                vmem_limit_bytes=LIMIT, collective_id=0, has_side_effects=True
            ),
            name="whole",
        )(taps, counts, pair_blocks.T, owners.T, *operands)
        by_lane = pl.pallas_call(
            owner_kernel,
            out_shape=jax.ShapeDtypeStruct((CAP, lanes // groups, NLAG), jnp.float32),
            in_specs=[VMEM, pl.BlockSpec(memory_space=pl.ANY)],
            out_specs=pl.BlockSpec(memory_space=pl.ANY),
            scratch_shapes=[
                pltpu.VMEM((CAP // 2, devices, 2 * width, 128), bf16),
                pltpu.VMEM((CAP, lanes // groups, NLAG), jnp.float32),
                pltpu.SemaphoreType.DMA((CAP // 2,)),
                pltpu.SemaphoreType.DMA((CAP // 2,)),
            ],
            compiler_params=pltpu.CompilerParams(vmem_limit_bytes=LAST_LIMIT),
            name="owner",
        )(jnp.asarray(inverse.T), moved)
        return by_lane.transpose(0, 2, 1)
    params = pltpu.CompilerParams(vmem_limit_bytes=LIMIT)
    white = pl.pallas_call(
        functools.partial(front_kernel, block, segs),
        out_shape=jax.ShapeDtypeStruct((2 * nfreq, rows), bf16),
        in_specs=[VMEM, SMEM, VMEM, VMEM],
        out_specs=VMEM,
        scratch_shapes=[pltpu.VMEM((seglen, rows), bf16)],
        compiler_params=params,
        name="front",
    )(taps, counts, flat, forward)
    white = white.reshape(2, devices, width, rows).transpose(1, 0, 2, 3)
    bands = lax.all_to_all(white.reshape(devices, 2 * width, rows), AXES, 0, 0, tiled=True)
    stacked = cross_plain(bands, counts, pair_blocks, owners, nsta, groups, segs, width)
    moved = lax.all_to_all(stacked, AXES, 0, 0, tiled=True)
    return pl.pallas_call(
        last_kernel,
        out_shape=jax.ShapeDtypeStruct((CAP, NLAG, lanes // groups), jnp.float32),
        in_specs=[VMEM, VMEM],
        out_specs=VMEM,
        compiler_params=params,
        name="last",
    )(jnp.asarray(inverse), moved.reshape(2 * nfreq, CAP * lanes // groups))


def solution(mesh):
    in_specs = (P("sta", "seg", None), P(), P(), P(), P())
    out_specs = P("sta", None, "seg")
    return jax.shard_map(local, mesh=mesh, in_specs=in_specs, out_specs=out_specs, check_vma=False)
```

```python
import functools
import math

import jax
import jax.numpy as jnp
import ml_dtypes
import numpy as np
from jax import lax
from jax.experimental import pallas as pl
from jax.experimental.pallas import tpu as pltpu
from jax.sharding import PartitionSpec as P

DEC = 4
TAPS = 32
NLAG = 512
CAP = 4
WATER = 0.1
TINY = 1e-06
AXES = ("sta", "seg")
EARLY_SIDES = 1
VMEM = pl.BlockSpec(memory_space=pltpu.VMEM)
SMEM = pl.BlockSpec(memory_space=pltpu.SMEM)
LIMIT = 60 * 2**20


def forward_rows(seglen):
    phase = np.arange(seglen // 2)[:, None] * np.arange(seglen)[None, :] % seglen
    angle = phase * (2.0 * math.pi / seglen)
    both = np.concatenate([np.cos(angle), -np.sin(angle)], axis=0)
    return both.astype(np.float32).astype(ml_dtypes.bfloat16)


def inverse_rows(seglen, nlag, width):
    nfreq = seglen // 2
    lag = np.arange(nlag) - nlag // 2
    angle = (lag[:, None] * np.arange(nfreq)[None, :] % seglen) * (2.0 * math.pi / seglen)
    scale = 1.0 / math.sqrt(nfreq)
    both = np.stack([np.cos(angle) * scale, -np.sin(angle) * scale], axis=1)
    both = both.reshape(nlag, 2, nfreq // width, width).transpose(0, 2, 1, 3)
    return both.reshape(nlag, 2 * nfreq).astype(np.float32).astype(ml_dtypes.bfloat16)


def spread_tables(block, segs):
    eye = np.einsum("ai,sz->aszi", np.eye(block), np.eye(segs)).reshape(block * segs, segs, block)
    some = 128 // block
    by_i = np.repeat(eye, block, axis=2).reshape(block * segs, segs, block // some, 128).transpose(2, 0, 1, 3)
    by_j = np.tile(eye, (1, 1, some))
    shape = (block * segs, segs * 128)
    return by_i.reshape((-1,) + shape).astype(ml_dtypes.bfloat16), by_j.reshape(shape).astype(ml_dtypes.bfloat16)


def fir_rows(taps_ref):
    tap_of = (
        DEC * lax.broadcasted_iota(jnp.int32, (64, 128), 0) - lax.broadcasted_iota(jnp.int32, (64, 128), 1) - 61
    )
    taps = taps_ref[...].astype(jnp.float32)
    tile = jnp.zeros((64, 128), jnp.float32)
    for k in range(TAPS):
        tile = jnp.where(tap_of == k, taps[:, k : k + 1], tile)
    tile = tile.astype(jnp.bfloat16)
    columns = []
    for t in range(1 + DEC):
        top = 32 * t - 48
        low, high = max(top, 0), min(top + 64, 128)
        rows = [tile[low - top : high - top]]
        if low:
            rows.insert(0, jnp.zeros((low, 128), jnp.bfloat16))
        if high < 128:
            rows.append(jnp.zeros((128 - high, 128), jnp.bfloat16))
        columns.append(jnp.concatenate(rows, axis=0))
    return jnp.concatenate(columns, axis=1)


def decimate(fir, rec_ref, samp_ref):
    span = 128 * DEC
    for b in range(rec_ref.shape[1] // span):
        low = max(b * span - 128, 0)
        window = rec_ref[:, low : (b + 1) * span]
        kept = fir if b else fir[:, 128:]
        dec = lax.dot_general(
            kept, window, (((1,), (1,)), ((), ())), preferred_element_type=jnp.float32
        )
        samp_ref[b * 128 : (b + 1) * 128, :] = dec.astype(jnp.bfloat16)


def whitened(block, segs, counts_ref, dft_ref, samp_ref):
    rows = block * segs
    nfreq = dft_ref.shape[0] // 2
    spectrum = jnp.dot(dft_ref[...], samp_ref[...], preferred_element_type=jnp.float32)
    real, imag = spectrum[:nfreq], spectrum[nfreq:]
    magnitude = jnp.sqrt(real * real + imag * imag)
    mean_level = jnp.sum(magnitude, axis=0, keepdims=True) * (1.0 / nfreq)
    divisor = magnitude + WATER * mean_level + TINY
    lane = lax.broadcasted_iota(jnp.int32, (1, rows), 1)
    first = lax.axis_index("sta") * block
    limit = jnp.zeros((1, rows), jnp.int32)
    for i in range(block):
        limit = jnp.where(lane // segs == i, counts_ref[first + i], limit)
    valid = (lax.axis_index("seg") * segs + lane % segs < limit).astype(jnp.float32)
    gain = valid / divisor
    return real * gain, imag * gain


def front_kernel(block, segs, taps_ref, counts_ref, rec_ref, dft_ref, out_ref, samp_ref):
    decimate(fir_rows(taps_ref), rec_ref, samp_ref)
    nfreq = dft_ref.shape[0] // 2
    real, imag = whitened(block, segs, counts_ref, dft_ref, samp_ref)
    out_ref[:nfreq, :] = real.astype(jnp.bfloat16)
    out_ref[nfreq:, :] = imag.astype(jnp.bfloat16)


def whole_kernel(
    block, segs, nsta, groups, taps_ref, counts_ref, pairs_ref, owners_ref, rec_hbm, dft_hbm, by_i_hbm, by_j_hbm, inv_hbm,
    out_hbm, out_ref, rec_ref, dft_ref, by_i_ref, by_j_ref, inv_ref, samp_ref, white_ref, band_ref, left_ref, right_ref,
    sums_ref, made_ref, factor_ref, stack_ref, moved_ref, part_ref, slot_ref, order_ref, table_sem, send_sem, recv_sem, send2_sem, recv2_sem,
):
    devices = nsta * groups
    lanes = block * block
    width = white_ref.shape[1] // 2
    npairs = owners_ref.shape[1]
    own_sta, own_seg = lax.axis_index("sta"), lax.axis_index("seg")
    me = own_sta * groups + own_seg

    def place(d):
        return {"sta": d // groups, "seg": d % groups}

    tables = [
        pltpu.make_async_copy(src, dst, table_sem.at[n])
        for n, (src, dst) in enumerate(
            (
                (rec_hbm, rec_ref),
                (dft_hbm, dft_ref),
                (by_i_hbm, by_i_ref),
                (by_j_hbm, by_j_ref),
                (inv_hbm, inv_ref),
            )
        )
    ]
    for table in tables:
        table.start()
    barrier = pltpu.get_barrier_semaphore()

    @pl.loop(1, devices)
    def _(k):
        pl.semaphore_signal(
            barrier, inc=1, device_id=place(lax.rem(me + k, devices)), device_id_type=pl.DeviceIdType.MESH
        )

    fir = fir_rows(taps_ref)
    tables[0].wait()
    decimate(fir, rec_ref, samp_ref)
    tables[1].wait()
    real, imag = whitened(block, segs, counts_ref, dft_ref, samp_ref)
    for d in range(devices):
        both = jnp.concatenate([part[d * width : (d + 1) * width] for part in (real, imag)], axis=0)
        white_ref[d] = both.astype(jnp.bfloat16)
    pl.semaphore_wait(barrier, devices - 1)

    def band_copy(to, landed):
        return pltpu.make_async_remote_copy(
            src_ref=white_ref.at[to],
            dst_ref=band_ref.at[landed],
            send_sem=send_sem.at[to],
            recv_sem=recv_sem.at[landed],
            device_id=place(to),
            device_id_type=pl.DeviceIdType.MESH,
        )

    def stack_copy(to, landed):
        return pltpu.make_async_remote_copy(
            src_ref=stack_ref.at[to],
            dst_ref=moved_ref.at[landed],
            send_sem=send2_sem.at[to],
            recv_sem=recv2_sem.at[landed],
            device_id=place(to),
            device_id_type=pl.DeviceIdType.MESH,
        )

    @pl.loop(1, devices)
    def _(k):
        band_copy(lax.rem(me + k, devices), me).start()

    band_ref[me] = white_ref[me]

    many, few = nsta // 2, nsta - 2
    near_half = own_sta // many
    far_half = 1 - near_half
    firsts = [pairs_ref[0, p] for p in range(npairs)]
    seconds = [pairs_ref[1, p] for p in range(npairs)]
    inside = [
        ((first // many == near_half) & (second // many == near_half)).astype(jnp.int32)
        for first, second in zip(firsts, seconds)
    ]
    count = sum(inside)
    before = jnp.int32(0)
    places, slots = [], []
    for p in range(npairs):
        places.append(jnp.where(inside[p] == 1, before, count + p - before))
        before = before + inside[p]
        rank = jnp.int32(0)
        for q in range(p):
            rank = rank + (owners_ref[0, q] == owners_ref[0, p]).astype(jnp.int32)
        slots.append(owners_ref[0, p] * CAP + rank)
    for q in range(nsta * CAP):
        pair = jnp.int32(npairs)
        for p in range(npairs):
            pair = jnp.where(slots[p] == q, places[p], pair)
        slot_ref[q] = pair
    for q in range(npairs):
        pair = jnp.int32(0)
        for p in range(1, npairs):
            pair = jnp.where(places[p] == q, p, pair)
        order_ref[q] = pair
    made_ref[npairs] = jnp.zeros(made_ref.shape[1:], jnp.bfloat16)

    halves = lanes // 128
    per_half = 128 // block
    lane = lax.broadcasted_iota(jnp.int32, (1, 128), 1)
    low = lax.broadcasted_iota(jnp.int32, (2 * width, 128), 1) < 64
    sides = list(range(halves))

    @pl.loop(0, npairs)
    def _(p):
        first, second = pairs_ref[0, p], pairs_ref[1, p]
        right_count = jnp.zeros((1, 128), jnp.int32)
        for i in range(block):
            right_count = jnp.where(lane % block == i, counts_ref[second * block + i], right_count)
        for side in range(halves):
            left_count = jnp.zeros((1, 128), jnp.int32)
            for i in range(per_half):
                here = counts_ref[first * block + side * per_half + i]
                left_count = jnp.where(lane // block == i, here, left_count)
            factor = 1.0 / jnp.minimum(left_count, right_count).astype(jnp.float32)
            factor_ref[side, p] = jnp.broadcast_to(factor, factor_ref.shape[2:])

    def expand(half, table, into):
        held = band_ref[pl.ds(half * many * groups, many * groups)].reshape(many * groups * 2 * width, -1)
        for s in range(0, segs, 2):
            wide = jnp.dot(held, table[:, s * 128 : s * 128 + 256], preferred_element_type=jnp.float32)
            wide = wide.reshape(many, groups * 2 * width, 256)
            into[pl.ds(half * many, many), s] = wide[:, :, :128]
            into[pl.ds(half * many, many), s + 1] = wide[:, :, 128:]

    def cross(side, low_pair, high_pair):
        @pl.loop(low_pair, high_pair)
        def _(n):
            p = order_ref[n]
            first, second = pairs_ref[0, p], pairs_ref[1, p]
            factor = factor_ref[side, p]
            for r in range(0, width, 8):
                sums = [jnp.zeros((8, 128), jnp.float32) for _ in range(8)]
                for s in range(segs):
                    for g in range(groups):
                        at = g * 2 * width + r
                        lr = left_ref[side, first, s, at : at + 8, :]
                        li = left_ref[side, first, s, at + width : at + width + 8, :]
                        rr = right_ref[second, s, at : at + 8, :]
                        ri = right_ref[second, s, at + width : at + width + 8, :]
                        m = g % 2 * 4
                        sums[m] += lr * rr
                        sums[m + 1] += li * ri
                        sums[m + 2] += li * rr
                        sums[m + 3] += lr * ri
                sums = [sums[m] + sums[m + 4] for m in range(4)]
                sums_ref[side, n, r : r + 8] = (sums[0] + sums[1]) * factor
                sums_ref[side, n, width + r : width + r + 8] = (sums[2] - sums[3]) * factor

    tables[2].wait()
    tables[3].wait()

    @pl.loop(1, many * groups)
    def _(k):
        src = near_half * many * groups + lax.rem(me + k, many * groups)
        band_copy(src, src).wait_recv()

    expand(near_half, by_j_ref, right_ref)
    for side in sides[:EARLY_SIDES]:
        expand(near_half, by_i_ref.at[side], left_ref.at[side])
        cross(side, 0, few)

    @pl.loop(0, many * groups)
    def _(k):
        src = far_half * many * groups + lax.rem(me + k, many * groups)
        band_copy(src, src).wait_recv()

    expand(far_half, by_j_ref, right_ref)
    for turn, side in enumerate(sides):
        expand(far_half, by_i_ref.at[side], left_ref.at[side])
        if turn >= EARLY_SIDES:
            expand(near_half, by_i_ref.at[side], left_ref.at[side])
            cross(side, 0, few)
        cross(side, few, npairs)
        every = sums_ref[side].reshape(npairs * 2 * width, 128)
        for n, turned in enumerate((every, pltpu.roll(every, 64, 1))):
            made_ref[:npairs, n] = turned.astype(jnp.bfloat16).reshape(npairs, 2 * width, 128)
        for k in range(nsta):
            owner = lax.rem(own_sta + 1 + k, nsta)
            to = owner * groups + 2 * side
            for half in range(CAP // 2):
                even, odd = slot_ref[owner * CAP + 2 * half], slot_ref[owner * CAP + 2 * half + 1]
                stack_ref[to, half] = jnp.where(low, made_ref[even, 0], made_ref[odd, 1])
                stack_ref[to + 1, half] = jnp.where(low, made_ref[even, 1], made_ref[odd, 0])

        @pl.loop(0, 2 * nsta)
        def _(k):
            to = lax.rem(own_sta + 1 + k // 2, nsta) * groups + 2 * side + k % 2

            @pl.when(to != me)
            def _():
                stack_copy(to, me).start()

    moved_ref[me] = stack_ref[me]
    tables[4].wait()
    span = many * groups

    @pl.loop(1, devices)
    def _(k):
        band_copy(lax.rem(me + k, devices), me).wait_send()

    def partial(half, h):
        held = moved_ref[pl.ds(half * span, span), h].reshape(span * 2 * width, 128)
        table = inv_ref[pl.ds(pl.multiple_of(half * span * 2 * width, 128), span * 2 * width)]
        return lax.dot_general(held, table, (((0,), (0,)), ((), ())), preferred_element_type=jnp.float32)

    @pl.loop(1, span)
    def _(k):
        src = near_half * span + lax.rem(me + k, span)
        stack_copy(src, src).wait_recv()

    for h in range(CAP // 2):
        part_ref[h] = partial(near_half, h)

    @pl.loop(0, span)
    def _(k):
        src = far_half * span + lax.rem(me + k, span)
        stack_copy(src, src).wait_recv()

    stores = []
    for h in range(CAP // 2):
        result = (part_ref[h] + partial(far_half, h)).astype(jnp.bfloat16)
        out_ref[2 * h] = result[:64]
        out_ref[2 * h + 1] = result[64:]
        stores.append(pltpu.make_async_copy(out_ref.at[pl.ds(2 * h, 2)], out_hbm.at[pl.ds(2 * h, 2)], table_sem.at[h]))
        stores[h].start()

    @pl.loop(1, devices)
    def _(k):
        stack_copy(lax.rem(me + k, devices), me).wait_send()

    for store in stores:
        store.wait()


def widen_kernel(from_hbm, to_hbm, from_ref, to_ref, in_sem, out_sem):
    loads = [pltpu.make_async_copy(from_hbm.at[n], from_ref.at[n], in_sem.at[n]) for n in range(CAP)]
    stores = [pltpu.make_async_copy(to_ref.at[n], to_hbm.at[n], out_sem.at[n]) for n in range(CAP)]
    for load in loads:
        load.start()
    for n in range(CAP):
        loads[n].wait()
        to_ref[n] = from_ref[n].astype(jnp.float32)
        stores[n].start()
    for store in stores:
        store.wait()


def cross_plain(bands, counts, pair_blocks, owners, nsta, groups, segs, width):
    owner_ids = owners[:, 0]
    position = jnp.arange(owner_ids.shape[0], dtype=jnp.int32)
    same = (owner_ids[:, None] == owner_ids[None, :]) & (position[None, :] < position[:, None])
    slot_of = owner_ids * CAP + jnp.sum(same.astype(jnp.int32), axis=1)
    block = counts.shape[0] // nsta
    hit = (slot_of[:, None] == jnp.arange(nsta * CAP, dtype=jnp.int32)[None, :]).astype(jnp.bfloat16)
    blocks = jnp.arange(nsta, dtype=jnp.int32)
    data = bands.reshape(nsta, groups, 2, width, block, segs)
    grid = counts.reshape(nsta, block).astype(jnp.float32)
    sides, limits = [], []
    for side in range(2):
        pick = (pair_blocks[:, side][:, None] == blocks[None, :]).astype(jnp.bfloat16)
        chosen = jnp.einsum("pn,ngufis->pgufis", pick, data, preferred_element_type=jnp.float32)
        sides.append(chosen.astype(jnp.bfloat16))
        limits.append(jnp.sum(jnp.where(pick[:, :, None] > 0, grid[None], 0.0), axis=1))
    left, right = sides
    common = jnp.minimum(limits[0][:, None, :, None], limits[1][:, None, None, :])
    dot = functools.partial(jnp.einsum, "pgfis,pgfjs->pfij", preferred_element_type=jnp.float32)
    real = dot(left[:, :, 0], right[:, :, 0]) + dot(left[:, :, 1], right[:, :, 1])
    imag = dot(left[:, :, 1], right[:, :, 0]) - dot(left[:, :, 0], right[:, :, 1])
    made = jnp.stack([real / common, imag / common], axis=1).astype(jnp.bfloat16)
    slots = jnp.einsum("pq,pufl->qufl", hit, made.reshape(made.shape[:3] + (block * block,)), preferred_element_type=jnp.float32)
    slots = slots.astype(jnp.bfloat16).reshape(nsta, CAP, 2, width, groups, block * block // groups)
    return slots.transpose(0, 4, 2, 3, 1, 5).reshape(nsta * groups, 2 * width, CAP * block * block // groups)


def last_kernel(inv_ref, stack_ref, out_ref):
    result = jnp.dot(inv_ref[...], stack_ref[...], preferred_element_type=jnp.float32)
    lanes = out_ref.shape[2]
    for c in range(out_ref.shape[0]):
        out_ref[c] = result[:, c * lanes : (c + 1) * lanes]


def local(records, fir_taps, counts, pair_blocks, owners):
    block, segs, raw = records.shape
    nsta, groups = lax.axis_size("sta"), lax.axis_size("seg")
    devices = nsta * groups
    seglen = raw // DEC
    nfreq = seglen // 2
    width = nfreq // devices
    rows = block * segs
    lanes = block * block
    fast = width % 16 == 0 and nsta == 8 and owners.shape[0] == 2 * nsta and lanes // groups == 64 and rows == 128
    bf16 = jnp.bfloat16

    taps = fir_taps.reshape(1, TAPS)
    flat = records.reshape(rows, raw)
    forward = jnp.asarray(forward_rows(seglen))
    inverse = inverse_rows(seglen, NLAG, width)
    if fast:
        by_i, by_j = (jnp.asarray(t) for t in spread_tables(block, segs))
        operands = (flat, forward, by_i, by_j, jnp.asarray(inverse.T))
        spread = (nsta, segs, groups * 2 * width, 128)
        bands = pltpu.VMEM((devices, 2 * width, rows), bf16)
        stacks = pltpu.VMEM((devices, CAP // 2, 2 * width, 128), bf16)
        by_lane = pl.pallas_call(
            functools.partial(whole_kernel, block, segs, nsta, groups),
            out_shape=jax.ShapeDtypeStruct((CAP, lanes // groups, NLAG), bf16),
            in_specs=[VMEM] + [SMEM] * 3 + [pl.BlockSpec(memory_space=pl.ANY)] * 5,
            out_specs=pl.BlockSpec(memory_space=pl.ANY),
            scratch_shapes=[
                pltpu.VMEM((CAP, lanes // groups, NLAG), bf16),
                *(pltpu.VMEM(x.shape, bf16) for x in operands),
                pltpu.VMEM((seglen, rows), bf16),
                bands,
                bands,
                pltpu.VMEM((lanes // 128,) + spread, jnp.float32),
                pltpu.VMEM(spread, jnp.float32),
                pltpu.VMEM((lanes // 128, owners.shape[0], 2 * width, 128), jnp.float32),
                pltpu.VMEM((owners.shape[0] + 1, 2, 2 * width, 128), bf16),
                pltpu.VMEM((lanes // 128, owners.shape[0], 8, 128), jnp.float32),
                stacks,
                stacks,
                pltpu.VMEM((CAP // 2, 128, NLAG), jnp.float32),
                pltpu.SMEM((nsta * CAP,), jnp.int32),
                pltpu.SMEM((owners.shape[0],), jnp.int32),
                pltpu.SemaphoreType.DMA((5,)),
                *(pltpu.SemaphoreType.DMA((devices)) for _ in range(4)),
            ],
            compiler_params=pltpu.CompilerParams(
                vmem_limit_bytes=LIMIT, collective_id=0, has_side_effects=True
            ),
            name="whole",
        )(taps, counts, pair_blocks.T, owners.T, *operands)
        by_lane = pl.pallas_call(
            widen_kernel,
            out_shape=jax.ShapeDtypeStruct(by_lane.shape, jnp.float32),
            in_specs=[pl.BlockSpec(memory_space=pl.ANY)],
            out_specs=pl.BlockSpec(memory_space=pl.ANY),
            scratch_shapes=[
                pltpu.VMEM(by_lane.shape, bf16),
                pltpu.VMEM(by_lane.shape, jnp.float32),
                pltpu.SemaphoreType.DMA((CAP,)),
                pltpu.SemaphoreType.DMA((CAP,)),
            ],
            compiler_params=pltpu.CompilerParams(vmem_limit_bytes=LIMIT),
            name="widen",
        )(by_lane)
        return by_lane.transpose(0, 2, 1)
    params = pltpu.CompilerParams(vmem_limit_bytes=LIMIT)
    white = pl.pallas_call(
        functools.partial(front_kernel, block, segs),
        out_shape=jax.ShapeDtypeStruct((2 * nfreq, rows), bf16),
        in_specs=[VMEM, SMEM, VMEM, VMEM],
        out_specs=VMEM,
        scratch_shapes=[pltpu.VMEM((seglen, rows), bf16)],
        compiler_params=params,
        name="front",
    )(taps, counts, flat, forward)
    white = white.reshape(2, devices, width, rows).transpose(1, 0, 2, 3)
    bands = lax.all_to_all(white.reshape(devices, 2 * width, rows), AXES, 0, 0, tiled=True)
    stacked = cross_plain(bands, counts, pair_blocks, owners, nsta, groups, segs, width)
    moved = lax.all_to_all(stacked, AXES, 0, 0, tiled=True)
    return pl.pallas_call(
        last_kernel,
        out_shape=jax.ShapeDtypeStruct((CAP, NLAG, lanes // groups), jnp.float32),
        in_specs=[VMEM, VMEM],
        out_specs=VMEM,
        compiler_params=params,
        name="last",
    )(jnp.asarray(inverse), moved.reshape(2 * nfreq, CAP * lanes // groups))


def solution(mesh):
    in_specs = (P("sta", "seg", None), P(), P(), P(), P())
    out_specs = P("sta", None, "seg")
    return jax.shard_map(local, mesh=mesh, in_specs=in_specs, out_specs=out_specs, check_vma=False)
```

```python
import functools
import math

import jax
import jax.numpy as jnp
import ml_dtypes
import numpy as np
from jax import lax
from jax.experimental import pallas as pl
from jax.experimental.pallas import tpu as pltpu
from jax.sharding import PartitionSpec as P

DEC = 4
TAPS = 32
NLAG = 512
CAP = 4
WATER = 0.1
TINY = 1e-06
AXES = ("sta", "seg")
EARLY_SIDES = 1
VMEM = pl.BlockSpec(memory_space=pltpu.VMEM)
SMEM = pl.BlockSpec(memory_space=pltpu.SMEM)
LIMIT = 60 * 2**20


def forward_rows(seglen):
    phase = np.arange(seglen // 2)[:, None] * np.arange(seglen)[None, :] % seglen
    angle = phase * (2.0 * math.pi / seglen)
    both = np.concatenate([np.cos(angle), -np.sin(angle)], axis=0)
    return both.astype(np.float32).astype(ml_dtypes.bfloat16)


def inverse_rows(seglen, nlag, width):
    nfreq = seglen // 2
    lag = np.arange(nlag) - nlag // 2
    angle = (lag[:, None] * np.arange(nfreq)[None, :] % seglen) * (2.0 * math.pi / seglen)
    scale = 1.0 / math.sqrt(nfreq)
    both = np.stack([np.cos(angle) * scale, -np.sin(angle) * scale], axis=1)
    both = both.reshape(nlag, 2, nfreq // width, width).transpose(0, 2, 1, 3)
    return both.reshape(nlag, 2 * nfreq).astype(np.float32).astype(ml_dtypes.bfloat16)


def spread_tables(block, segs):
    eye = np.einsum("ai,sz->aszi", np.eye(block), np.eye(segs)).reshape(block * segs, segs, block)
    some = 128 // block
    by_i = np.repeat(eye, block, axis=2).reshape(block * segs, segs, block // some, 128).transpose(2, 0, 1, 3)
    by_j = np.tile(eye, (1, 1, some))
    shape = (block * segs, segs * 128)
    return by_i.reshape((-1,) + shape).astype(ml_dtypes.bfloat16), by_j.reshape(shape).astype(ml_dtypes.bfloat16)


def fir_rows(taps_ref):
    tap_of = (
        DEC * lax.broadcasted_iota(jnp.int32, (64, 128), 0) - lax.broadcasted_iota(jnp.int32, (64, 128), 1) - 61
    )
    taps = taps_ref[...].astype(jnp.float32)
    tile = jnp.zeros((64, 128), jnp.float32)
    for k in range(TAPS):
        tile = jnp.where(tap_of == k, taps[:, k : k + 1], tile)
    tile = tile.astype(jnp.bfloat16)
    columns = []
    for t in range(1 + DEC):
        top = 32 * t - 48
        low, high = max(top, 0), min(top + 64, 128)
        rows = [tile[low - top : high - top]]
        if low:
            rows.insert(0, jnp.zeros((low, 128), jnp.bfloat16))
        if high < 128:
            rows.append(jnp.zeros((128 - high, 128), jnp.bfloat16))
        columns.append(jnp.concatenate(rows, axis=0))
    return jnp.concatenate(columns, axis=1)


def decimate(fir, rec_ref, samp_ref):
    span = 128 * DEC
    for b in range(rec_ref.shape[1] // span):
        low = max(b * span - 128, 0)
        window = rec_ref[:, low : (b + 1) * span]
        kept = fir if b else fir[:, 128:]
        dec = lax.dot_general(
            kept, window, (((1,), (1,)), ((), ())), preferred_element_type=jnp.float32
        )
        samp_ref[b * 128 : (b + 1) * 128, :] = dec.astype(jnp.bfloat16)


def whitened(block, segs, counts_ref, dft_ref, samp_ref):
    rows = block * segs
    nfreq = dft_ref.shape[0] // 2
    spectrum = jnp.dot(dft_ref[...], samp_ref[...], preferred_element_type=jnp.float32)
    real, imag = spectrum[:nfreq], spectrum[nfreq:]
    magnitude = jnp.sqrt(real * real + imag * imag)
    mean_level = jnp.sum(magnitude, axis=0, keepdims=True) * (1.0 / nfreq)
    divisor = magnitude + WATER * mean_level + TINY
    lane = lax.broadcasted_iota(jnp.int32, (1, rows), 1)
    first = lax.axis_index("sta") * block
    limit = jnp.zeros((1, rows), jnp.int32)
    for i in range(block):
        limit = jnp.where(lane // segs == i, counts_ref[first + i], limit)
    valid = (lax.axis_index("seg") * segs + lane % segs < limit).astype(jnp.float32)
    gain = valid / divisor
    return real * gain, imag * gain


def front_kernel(block, segs, taps_ref, counts_ref, rec_ref, dft_ref, out_ref, samp_ref):
    decimate(fir_rows(taps_ref), rec_ref, samp_ref)
    nfreq = dft_ref.shape[0] // 2
    real, imag = whitened(block, segs, counts_ref, dft_ref, samp_ref)
    out_ref[:nfreq, :] = real.astype(jnp.bfloat16)
    out_ref[nfreq:, :] = imag.astype(jnp.bfloat16)


def whole_kernel(
    block, segs, nsta, groups, taps_ref, counts_ref, pairs_ref, owners_ref, rec_hbm, dft_hbm, by_i_hbm, by_j_hbm, inv_hbm,
    out_hbm, out_ref, rec_ref, dft_ref, by_i_ref, by_j_ref, inv_ref, samp_ref, white_ref, band_ref, left_ref, right_ref,
    sums_ref, made_ref, factor_ref, stack_ref, moved_ref, part_ref, slot_ref, order_ref, table_sem, send_sem, recv_sem, send2_sem, recv2_sem,
):
    devices = nsta * groups
    lanes = block * block
    width = white_ref.shape[1] // 2
    npairs = owners_ref.shape[1]
    own_sta, own_seg = lax.axis_index("sta"), lax.axis_index("seg")
    me = own_sta * groups + own_seg

    def place(d):
        return {"sta": d // groups, "seg": d % groups}

    tables = [
        pltpu.make_async_copy(src, dst, table_sem.at[n])
        for n, (src, dst) in enumerate(
            (
                (rec_hbm, rec_ref),
                (dft_hbm, dft_ref),
                (by_i_hbm, by_i_ref),
                (by_j_hbm, by_j_ref),
                (inv_hbm, inv_ref),
            )
        )
    ]
    for table in tables:
        table.start()
    barrier = pltpu.get_barrier_semaphore()

    @pl.loop(1, devices, unroll=True)
    def _(k):
        pl.semaphore_signal(
            barrier, inc=1, device_id=place(lax.rem(me + k, devices)), device_id_type=pl.DeviceIdType.MESH
        )

    fir = fir_rows(taps_ref)
    tables[0].wait()
    decimate(fir, rec_ref, samp_ref)
    tables[1].wait()
    real, imag = whitened(block, segs, counts_ref, dft_ref, samp_ref)
    for d in range(devices):
        both = jnp.concatenate([part[d * width : (d + 1) * width] for part in (real, imag)], axis=0)
        white_ref[d] = both.astype(jnp.bfloat16)
    pl.semaphore_wait(barrier, devices - 1)

    def band_copy(to, landed):
        return pltpu.make_async_remote_copy(
            src_ref=white_ref.at[to],
            dst_ref=band_ref.at[landed],
            send_sem=send_sem.at[to],
            recv_sem=recv_sem.at[landed],
            device_id=place(to),
            device_id_type=pl.DeviceIdType.MESH,
        )

    def stack_copy(to, landed):
        return pltpu.make_async_remote_copy(
            src_ref=stack_ref.at[to],
            dst_ref=moved_ref.at[landed],
            send_sem=send2_sem.at[to],
            recv_sem=recv2_sem.at[landed],
            device_id=place(to),
            device_id_type=pl.DeviceIdType.MESH,
        )

    @pl.loop(1, devices, unroll=True)
    def _(k):
        band_copy(lax.rem(me + k, devices), me).start()

    band_ref[me] = white_ref[me]

    many, few = nsta // 2, nsta - 2
    near_half = own_sta // many
    far_half = 1 - near_half
    firsts = [pairs_ref[0, p] for p in range(npairs)]
    seconds = [pairs_ref[1, p] for p in range(npairs)]
    inside = [
        ((first // many == near_half) & (second // many == near_half)).astype(jnp.int32)
        for first, second in zip(firsts, seconds)
    ]
    count = sum(inside)
    before = jnp.int32(0)
    places, slots = [], []
    for p in range(npairs):
        places.append(jnp.where(inside[p] == 1, before, count + p - before))
        before = before + inside[p]
        rank = jnp.int32(0)
        for q in range(p):
            rank = rank + (owners_ref[0, q] == owners_ref[0, p]).astype(jnp.int32)
        slots.append(owners_ref[0, p] * CAP + rank)
    for q in range(nsta * CAP):
        pair = jnp.int32(npairs)
        for p in range(npairs):
            pair = jnp.where(slots[p] == q, places[p], pair)
        slot_ref[q] = pair
    for q in range(npairs):
        pair = jnp.int32(0)
        for p in range(1, npairs):
            pair = jnp.where(places[p] == q, p, pair)
        order_ref[q] = pair
    made_ref[npairs] = jnp.zeros(made_ref.shape[1:], jnp.bfloat16)

    halves = lanes // 128
    per_half = 128 // block
    lane = lax.broadcasted_iota(jnp.int32, (1, 128), 1)
    low = lax.broadcasted_iota(jnp.int32, (2 * width, 128), 1) < 64
    sides = list(range(halves))

    @pl.loop(0, npairs)
    def _(p):
        first, second = pairs_ref[0, p], pairs_ref[1, p]
        right_count = jnp.zeros((1, 128), jnp.int32)
        for i in range(block):
            right_count = jnp.where(lane % block == i, counts_ref[second * block + i], right_count)
        for side in range(halves):
            left_count = jnp.zeros((1, 128), jnp.int32)
            for i in range(per_half):
                here = counts_ref[first * block + side * per_half + i]
                left_count = jnp.where(lane // block == i, here, left_count)
            factor = 1.0 / jnp.minimum(left_count, right_count).astype(jnp.float32)
            factor_ref[side, p] = jnp.broadcast_to(factor, factor_ref.shape[2:])

    def expand(half, table, into):
        held = band_ref[pl.ds(half * many * groups, many * groups)].reshape(many * groups * 2 * width, -1)
        for s in range(0, segs, 2):
            wide = jnp.dot(held, table[:, s * 128 : s * 128 + 256], preferred_element_type=jnp.float32)
            wide = wide.reshape(many, groups * 2 * width, 256)
            into[pl.ds(half * many, many), s] = wide[:, :, :128]
            into[pl.ds(half * many, many), s + 1] = wide[:, :, 128:]

    def cross(side, low_pair, high_pair):
        @pl.loop(low_pair, high_pair, unroll=2)
        def _(n):
            p = order_ref[n]
            first, second = pairs_ref[0, p], pairs_ref[1, p]
            factor = factor_ref[side, p]
            for r in range(0, width, 8):
                sums = [jnp.zeros((8, 128), jnp.float32) for _ in range(8)]
                for s in range(segs):
                    for g in range(groups):
                        at = g * 2 * width + r
                        lr = left_ref[side, first, s, at : at + 8, :]
                        li = left_ref[side, first, s, at + width : at + width + 8, :]
                        rr = right_ref[second, s, at : at + 8, :]
                        ri = right_ref[second, s, at + width : at + width + 8, :]
                        m = g % 2 * 4
                        sums[m] += lr * rr
                        sums[m + 1] += li * ri
                        sums[m + 2] += li * rr
                        sums[m + 3] += lr * ri
                sums = [sums[m] + sums[m + 4] for m in range(4)]
                sums_ref[side, n, r : r + 8] = (sums[0] + sums[1]) * factor
                sums_ref[side, n, width + r : width + r + 8] = (sums[2] - sums[3]) * factor

    tables[2].wait()
    tables[3].wait()

    @pl.loop(1, many * groups)
    def _(k):
        src = near_half * many * groups + lax.rem(me + k, many * groups)
        band_copy(src, src).wait_recv()

    expand(near_half, by_j_ref, right_ref)
    for side in sides[:EARLY_SIDES]:
        expand(near_half, by_i_ref.at[side], left_ref.at[side])
        cross(side, 0, few)

    @pl.loop(0, many * groups)
    def _(k):
        src = far_half * many * groups + lax.rem(me + k, many * groups)
        band_copy(src, src).wait_recv()

    expand(far_half, by_j_ref, right_ref)
    for turn, side in enumerate(sides):
        expand(far_half, by_i_ref.at[side], left_ref.at[side])
        if turn >= EARLY_SIDES:
            expand(near_half, by_i_ref.at[side], left_ref.at[side])
            cross(side, 0, few)
        cross(side, few, npairs)
        every = sums_ref[side].reshape(npairs * 2 * width, 128)
        for n, turned in enumerate((every, pltpu.roll(every, 64, 1))):
            made_ref[:npairs, n] = turned.astype(jnp.bfloat16).reshape(npairs, 2 * width, 128)
        for k in range(nsta):
            owner = lax.rem(own_sta + 1 + k, nsta)
            to = owner * groups + 2 * side
            for half in range(CAP // 2):
                even, odd = slot_ref[owner * CAP + 2 * half], slot_ref[owner * CAP + 2 * half + 1]
                stack_ref[to, half] = jnp.where(low, made_ref[even, 0], made_ref[odd, 1])
                stack_ref[to + 1, half] = jnp.where(low, made_ref[even, 1], made_ref[odd, 0])

        @pl.loop(0, 2 * nsta)
        def _(k):
            to = lax.rem(own_sta + 1 + k // 2, nsta) * groups + 2 * side + k % 2

            @pl.when(to != me)
            def _():
                stack_copy(to, me).start()

    moved_ref[me] = stack_ref[me]
    tables[4].wait()
    span = many * groups

    @pl.loop(1, devices)
    def _(k):
        band_copy(lax.rem(me + k, devices), me).wait_send()

    def partial(half, h):
        held = moved_ref[pl.ds(half * span, span), h].reshape(span * 2 * width, 128)
        table = inv_ref[pl.ds(pl.multiple_of(half * span * 2 * width, 128), span * 2 * width)]
        return lax.dot_general(held, table, (((0,), (0,)), ((), ())), preferred_element_type=jnp.float32)

    @pl.loop(1, span)
    def _(k):
        src = near_half * span + lax.rem(me + k, span)
        stack_copy(src, src).wait_recv()

    for h in range(CAP // 2):
        part_ref[h] = partial(near_half, h)

    @pl.loop(0, span)
    def _(k):
        src = far_half * span + lax.rem(me + k, span)
        stack_copy(src, src).wait_recv()

    stores = []
    for h in range(CAP // 2):
        result = (part_ref[h] + partial(far_half, h)).astype(jnp.bfloat16)
        out_ref[2 * h] = result[:64]
        out_ref[2 * h + 1] = result[64:]
        stores.append(pltpu.make_async_copy(out_ref.at[pl.ds(2 * h, 2)], out_hbm.at[pl.ds(2 * h, 2)], table_sem.at[h]))
        stores[h].start()

    @pl.loop(1, devices)
    def _(k):
        stack_copy(lax.rem(me + k, devices), me).wait_send()

    for store in stores:
        store.wait()


def widen_kernel(from_hbm, to_hbm, from_ref, to_ref, in_sem, out_sem):
    loads = [pltpu.make_async_copy(from_hbm.at[n], from_ref.at[n], in_sem.at[n]) for n in range(CAP)]
    stores = [pltpu.make_async_copy(to_ref.at[n], to_hbm.at[n], out_sem.at[n]) for n in range(CAP)]
    for load in loads:
        load.start()
    for n in range(CAP):
        loads[n].wait()
        to_ref[n] = from_ref[n].astype(jnp.float32)
        stores[n].start()
    for store in stores:
        store.wait()


def cross_plain(bands, counts, pair_blocks, owners, nsta, groups, segs, width):
    owner_ids = owners[:, 0]
    position = jnp.arange(owner_ids.shape[0], dtype=jnp.int32)
    same = (owner_ids[:, None] == owner_ids[None, :]) & (position[None, :] < position[:, None])
    slot_of = owner_ids * CAP + jnp.sum(same.astype(jnp.int32), axis=1)
    block = counts.shape[0] // nsta
    hit = (slot_of[:, None] == jnp.arange(nsta * CAP, dtype=jnp.int32)[None, :]).astype(jnp.bfloat16)
    blocks = jnp.arange(nsta, dtype=jnp.int32)
    data = bands.reshape(nsta, groups, 2, width, block, segs)
    grid = counts.reshape(nsta, block).astype(jnp.float32)
    sides, limits = [], []
    for side in range(2):
        pick = (pair_blocks[:, side][:, None] == blocks[None, :]).astype(jnp.bfloat16)
        chosen = jnp.einsum("pn,ngufis->pgufis", pick, data, preferred_element_type=jnp.float32)
        sides.append(chosen.astype(jnp.bfloat16))
        limits.append(jnp.sum(jnp.where(pick[:, :, None] > 0, grid[None], 0.0), axis=1))
    left, right = sides
    common = jnp.minimum(limits[0][:, None, :, None], limits[1][:, None, None, :])
    dot = functools.partial(jnp.einsum, "pgfis,pgfjs->pfij", preferred_element_type=jnp.float32)
    real = dot(left[:, :, 0], right[:, :, 0]) + dot(left[:, :, 1], right[:, :, 1])
    imag = dot(left[:, :, 1], right[:, :, 0]) - dot(left[:, :, 0], right[:, :, 1])
    made = jnp.stack([real / common, imag / common], axis=1).astype(jnp.bfloat16)
    slots = jnp.einsum("pq,pufl->qufl", hit, made.reshape(made.shape[:3] + (block * block,)), preferred_element_type=jnp.float32)
    slots = slots.astype(jnp.bfloat16).reshape(nsta, CAP, 2, width, groups, block * block // groups)
    return slots.transpose(0, 4, 2, 3, 1, 5).reshape(nsta * groups, 2 * width, CAP * block * block // groups)


def last_kernel(inv_ref, stack_ref, out_ref):
    result = jnp.dot(inv_ref[...], stack_ref[...], preferred_element_type=jnp.float32)
    lanes = out_ref.shape[2]
    for c in range(out_ref.shape[0]):
        out_ref[c] = result[:, c * lanes : (c + 1) * lanes]


def local(records, fir_taps, counts, pair_blocks, owners):
    block, segs, raw = records.shape
    nsta, groups = lax.axis_size("sta"), lax.axis_size("seg")
    devices = nsta * groups
    seglen = raw // DEC
    nfreq = seglen // 2
    width = nfreq // devices
    rows = block * segs
    lanes = block * block
    fast = width % 16 == 0 and nsta == 8 and owners.shape[0] == 2 * nsta and lanes // groups == 64 and rows == 128
    bf16 = jnp.bfloat16

    taps = fir_taps.reshape(1, TAPS)
    flat = records.reshape(rows, raw)
    forward = jnp.asarray(forward_rows(seglen))
    inverse = inverse_rows(seglen, NLAG, width)
    if fast:
        by_i, by_j = (jnp.asarray(t) for t in spread_tables(block, segs))
        operands = (flat, forward, by_i, by_j, jnp.asarray(inverse.T))
        spread = (nsta, segs, groups * 2 * width, 128)
        bands = pltpu.VMEM((devices, 2 * width, rows), bf16)
        stacks = pltpu.VMEM((devices, CAP // 2, 2 * width, 128), bf16)
        by_lane = pl.pallas_call(
            functools.partial(whole_kernel, block, segs, nsta, groups),
            out_shape=jax.ShapeDtypeStruct((CAP, lanes // groups, NLAG), bf16),
            in_specs=[VMEM] + [SMEM] * 3 + [pl.BlockSpec(memory_space=pl.ANY)] * 5,
            out_specs=pl.BlockSpec(memory_space=pl.ANY),
            scratch_shapes=[
                pltpu.VMEM((CAP, lanes // groups, NLAG), bf16),
                *(pltpu.VMEM(x.shape, bf16) for x in operands),
                pltpu.VMEM((seglen, rows), bf16),
                bands,
                bands,
                pltpu.VMEM((lanes // 128,) + spread, jnp.float32),
                pltpu.VMEM(spread, jnp.float32),
                pltpu.VMEM((lanes // 128, owners.shape[0], 2 * width, 128), jnp.float32),
                pltpu.VMEM((owners.shape[0] + 1, 2, 2 * width, 128), bf16),
                pltpu.VMEM((lanes // 128, owners.shape[0], 8, 128), jnp.float32),
                stacks,
                stacks,
                pltpu.VMEM((CAP // 2, 128, NLAG), jnp.float32),
                pltpu.SMEM((nsta * CAP,), jnp.int32),
                pltpu.SMEM((owners.shape[0],), jnp.int32),
                pltpu.SemaphoreType.DMA((5,)),
                *(pltpu.SemaphoreType.DMA((devices)) for _ in range(4)),
            ],
            compiler_params=pltpu.CompilerParams(
                vmem_limit_bytes=LIMIT, collective_id=0, has_side_effects=True
            ),
            name="whole",
        )(taps, counts, pair_blocks.T, owners.T, *operands)
        by_lane = pl.pallas_call(
            widen_kernel,
            out_shape=jax.ShapeDtypeStruct(by_lane.shape, jnp.float32),
            in_specs=[pl.BlockSpec(memory_space=pl.ANY)],
            out_specs=pl.BlockSpec(memory_space=pl.ANY),
            scratch_shapes=[
                pltpu.VMEM(by_lane.shape, bf16),
                pltpu.VMEM(by_lane.shape, jnp.float32),
                pltpu.SemaphoreType.DMA((CAP,)),
                pltpu.SemaphoreType.DMA((CAP,)),
            ],
            compiler_params=pltpu.CompilerParams(vmem_limit_bytes=LIMIT),
            name="widen",
        )(by_lane)
        return by_lane.transpose(0, 2, 1)
    params = pltpu.CompilerParams(vmem_limit_bytes=LIMIT)
    white = pl.pallas_call(
        functools.partial(front_kernel, block, segs),
        out_shape=jax.ShapeDtypeStruct((2 * nfreq, rows), bf16),
        in_specs=[VMEM, SMEM, VMEM, VMEM],
        out_specs=VMEM,
        scratch_shapes=[pltpu.VMEM((seglen, rows), bf16)],
        compiler_params=params,
        name="front",
    )(taps, counts, flat, forward)
    white = white.reshape(2, devices, width, rows).transpose(1, 0, 2, 3)
    bands = lax.all_to_all(white.reshape(devices, 2 * width, rows), AXES, 0, 0, tiled=True)
    stacked = cross_plain(bands, counts, pair_blocks, owners, nsta, groups, segs, width)
    moved = lax.all_to_all(stacked, AXES, 0, 0, tiled=True)
    return pl.pallas_call(
        last_kernel,
        out_shape=jax.ShapeDtypeStruct((CAP, NLAG, lanes // groups), jnp.float32),
        in_specs=[VMEM, VMEM],
        out_specs=VMEM,
        compiler_params=params,
        name="last",
    )(jnp.asarray(inverse), moved.reshape(2 * nfreq, CAP * lanes // groups))


def solution(mesh):
    in_specs = (P("sta", "seg", None), P(), P(), P(), P())
    out_specs = P("sta", None, "seg")
    return jax.shard_map(local, mesh=mesh, in_specs=in_specs, out_specs=out_specs, check_vma=False)
```
